128 devices in a mesh: gx: 16 (over y, z), gy: 8 (over x, core).
Axes of the slice: x: 4, y: 4, z: 4, core: 2. Of those that a mesh axis runs over, the one named last changes fastest.
Arguments:
- populations: float32 [19, 128, 256, 256], P(None, 'gx', 'gy'), as said below
- displacement: float32 [3, 524288], P(None, ('gx', 'gy')), may hold values from -6 to 6
- offsets: float32 [3, 524288], P(None, ('gx', 'gy')), may hold values from 0 to 1
- cell_local: int32 [3, 524288], P(None, ('gx', 'gy')), may hold values from 0 to 254, as said below
- destination: int32 [524288, 1], P(('gx', 'gy')), may hold values from 0 to 127; in each aligned block of 4096 rows (0 to 4095, 4096 to 8191, ...) at most 128 rows name the same one
- triangles: int32 [1048576, 3], P(('gx', 'gy')), may hold values from 0 to 4095, as said below
- stiffness: float32 [1048576], P(('gx', 'gy')), may hold values from 0.05 to 0.5
Outputs:
- populations_next: float32 [19, 128, 256, 256], P(None, 'gx', 'gy')
- marker_velocity: float32 [3, 524288], P(None, ('gx', 'gy'))
The draws below stay inside these ranges and needn't reach their ends.
Inputs may be any that keep to these rules, and one draw needn't show every extreme that they name: `cell_local`: x below 7, y below 31, z below 255, so that all eight corners lie in the marker's tile. `destination`: at most 128 markers of one partition name the same tile; some partition sends exactly 128 to one tile. `triangles`: the three numbers of a triangle differ. `populations`: each population lies between 0.4 and 1.6 times its lattice weight.
All inputs are finite; a program needn't handle non-finite values.
Results may differ from the reference program's by a relative error of at most 0.00019.
Values sent between devices are 32-bit elements; how exact they have to be, the bound alone decides.
No kernel may reach another device: no remote copies, remote signals or barrier semaphores. Data moves between devices by JAX's collectives and lax.ppermute only.
A program may use at most 192 MiB of HBM per device.

```python
import math
import jax
import jax.numpy as jnp
import numpy as np

CX = 8
CY = 32
CZ = 256
M_DEV = 4096
CAP = 128
TRI_DEV = 8192
NX = 128
NY = 256
MARKERS = 524288
TRIS = 1048576
N_GY = 8
DEVICES = 128


WEIGHT_DRAW = np.array([1.0 / 3.0] + [1.0 / 18.0] * 6 + [1.0 / 36.0] * 12, dtype=np.float32)


def draw_populations(key, part):
    key = jax.random.fold_in(key, 11)
    shape = (19, NX, NY, CZ)
    weight = jnp.asarray(WEIGHT_DRAW).reshape(19, 1, 1, 1)
    noise = jax.random.uniform(key, shape, jnp.float32, 0.4, 1.6)
    return weight * noise


def draw_cell_local(key, part):
    key = jax.random.fold_in(key, 23)
    keys = jax.random.split(key, 3)
    along_x = jax.random.randint(keys[0], (MARKERS,), 0, CX - 1, dtype=jnp.int32)
    along_y = jax.random.randint(keys[1], (MARKERS,), 0, CY - 1, dtype=jnp.int32)
    along_z = jax.random.randint(keys[2], (MARKERS,), 0, CZ - 1, dtype=jnp.int32)
    return jnp.stack([along_x, along_y, along_z])


def draw_triangles(key, part):
    key = jax.random.fold_in(key, 37)
    keys = jax.random.split(key, 3)
    half = M_DEV // 2
    first = jax.random.randint(keys[0], (TRIS,), 0, M_DEV, dtype=jnp.int32)
    step_one = jax.random.randint(keys[1], (TRIS,), 1, half, dtype=jnp.int32)
    step_two = jax.random.randint(keys[2], (TRIS,), half, M_DEV, dtype=jnp.int32)
    second = (first + step_one) % M_DEV
    third = (first + step_two) % M_DEV
    return jnp.stack([first, second, third], axis=1)


def steps_of(rng, shape, cuts, smallest, top_value):
    loudness, own = 1.0, jax.random.fold_in(rng, 6)
    for dim, shards_of in cuts:
        draws = jnp.exp(jax.random.uniform(jax.random.fold_in(own, dim), (shards_of,), jnp.float32, smallest / len(cuts), top_value / len(cuts)))
        loudness = loudness * jnp.repeat(draws, shape[dim] // shards_of).reshape([-1 if axis == dim else 1 for axis in range(len(shape))])
    return loudness


def deal_out(key, own, number, rows, amount, top, most, slope):
    order = jax.random.permutation(key, amount)
    heavy_load, usual = portions_of(amount, rows * top, most, slope, True), portions_of(amount, rows * top, most, slope, False)
    places = jnp.arange(amount)

    def named(lengths, offset_by):
        used = int((lengths > 0).sum())
        fixed = max(1, used // 4)
        shifted = fixed + (places - fixed + offset_by * (used - fixed)) % max(1, amount - fixed)
        return jnp.zeros((amount,), jnp.int32).at[order[jnp.where(places < fixed, places, shifted)]].set(jnp.asarray(lengths, jnp.int32))

    lengths = jnp.where(number % 4 == 0, named(heavy_load, number // 4), named(usual, number - number // 4 - 1))
    mixed = jax.random.permutation(jax.random.fold_in(own, 3), amount)
    giver, receiver = mixed[0:amount // 2 * 2:2], mixed[1:amount // 2 * 2:2]
    slack = jnp.minimum(lengths[giver] - 1, most - lengths[receiver]) // 2
    slack = jnp.where((giver == order[0]) | (receiver == order[0]) | (lengths[receiver] == 0), 0, jnp.maximum(slack, 0))
    shifted = jax.random.randint(jax.random.fold_in(own, 4), (amount // 2,), 0, 1 << 20) % (slack + 1)
    lengths = lengths.at[giver].add(-shifted).at[receiver].add(shifted)
    items = jnp.searchsorted(jnp.cumsum(lengths), jnp.arange(rows * top), side="right").astype(jnp.int32)
    table = items.reshape(top, rows).T
    table = table[jax.random.permutation(jax.random.fold_in(own, 1), rows)]
    offset_by = jax.random.randint(jax.random.fold_in(own, 2), (rows, 1), 0, top)
    return jnp.take_along_axis(table, (jnp.arange(top)[None, :] + offset_by) % top, axis=1)


def portions_of(amount, total, most, lean, full):
    loads = [(1 << 20) // math.isqrt(rank ** lean) + 1 for rank in range(1, amount + 1)]
    largest = most if full else min(most, max(-(-total // amount), total * loads[0] // sum(loads)))
    least = 1 if total - largest >= amount - 1 else 0
    counts, rest = [largest] + [least] * (amount - 1), total - largest - least * (amount - 1)
    while rest > 0:
        movable = [i for i in range(1, amount) if counts[i] < largest] or [i for i in range(1, amount) if counts[i] < most]
        pool, remaining = sum([loads[i] for i in movable]), rest
        for i in movable:
            addition = min(most - counts[i], max(1, remaining * loads[i] // pool), rest)
            counts[i] = counts[i] + addition
            rest = rest - addition
    return np.array(counts)


def normal_values(stream_key, shape, deviation, most, cuts=(), kind=jnp.bfloat16):
    entries = jax.random.normal(stream_key, shape, jnp.float32) * deviation
    if len(cuts) > 0:
        entries = steps_of(stream_key, shape, cuts, -0.22, 0.18) * entries
    return jnp.clip(entries, min=-most, max=most).astype(kind)


def setup_inputs(seed: int = 0) -> dict:
    key_list = jax.random.split(jax.random.key(seed), 8)
    populations = draw_populations(jax.random.fold_in(key_list[7], 71), 0)
    displacement = normal_values(key_list[1], (3, MARKERS), 1.0, 6.0, ((1, 128),), jnp.float32)
    offsets = jnp.clip(1.0 * jax.random.uniform(key_list[2], (3, MARKERS), jnp.float32) ** steps_of(key_list[2], (3, MARKERS), ((1, 128),), -0.2, 0.2), 0.0, 1.0)
    cell_local = draw_cell_local(jax.random.fold_in(key_list[7], 71), 0)
    destination_keys = jax.random.split(jax.random.fold_in(key_list[4], 1), MARKERS // M_DEV)
    destination_turns = jax.random.permutation(jax.random.fold_in(key_list[4], 3), MARKERS // M_DEV)
    destination = jax.vmap(lambda own, number: deal_out(jax.random.fold_in(key_list[4], 2), own, number, M_DEV, DEVICES, 1, CAP, 2))(destination_keys, destination_turns).reshape((MARKERS, 1))
    triangles = draw_triangles(jax.random.fold_in(key_list[7], 71), 0)
    stiffness = jnp.clip(jnp.exp(math.log(0.5) - 2.3025851 * jax.random.uniform(key_list[6], (TRIS,), jnp.float32) ** steps_of(key_list[6], (TRIS,), ((0, 128),), -0.2, 0.2)), 0.05, 0.5)
    return dict(populations=populations, displacement=displacement, offsets=offsets, cell_local=cell_local, destination=destination, triangles=triangles, stiffness=stiffness)


LATTICE = np.array([[0, 0, 0], [1, 0, 0], [-1, 0, 0], [0, 1, 0], [0, -1, 0], [0, 0, 1], [0, 0, -1],
                    [1, 1, 0], [-1, -1, 0], [1, -1, 0], [-1, 1, 0], [1, 0, 1], [-1, 0, -1],
                    [1, 0, -1], [-1, 0, 1], [0, 1, 1], [0, -1, -1], [0, 1, -1], [0, -1, 1]])
LATTICE_WEIGHTS = [1.0 / 3.0] + [1.0 / 18.0] * 6 + [1.0 / 36.0] * 12
RELAX = 0.8


def membrane_force(displacement, vertices, stiffness, count):
    corner = displacement[:, vertices]
    total = jnp.sum(corner, axis=2, keepdims=True)
    terms = stiffness[None, :, None] * (total - 3.0 * corner)
    flat_terms = terms.reshape(3, -1)
    flat_vertices = vertices.reshape(-1)
    return jax.vmap(lambda row: jax.ops.segment_sum(row, flat_vertices, num_segments=count))(flat_terms)


def corner_terms(offsets, cell_flat, stride_x, stride_y):
    indices = []
    weights = []
    for step_x in (0, 1):
        for step_y in (0, 1):
            for step_z in (0, 1):
                weight_x = offsets[0] if step_x else 1.0 - offsets[0]
                weight_y = offsets[1] if step_y else 1.0 - offsets[1]
                weight_z = offsets[2] if step_z else 1.0 - offsets[2]
                weights.append(weight_x * weight_y * weight_z)
                indices.append(cell_flat + step_x * stride_x + step_y * stride_y + step_z)
    return jnp.stack(indices), jnp.stack(weights)


def collide(pops, force):
    rho = pops[0]
    for q in range(1, 19):
        rho = rho + pops[q]
    moments = []
    for axis_c in range(3):
        moment = jnp.zeros_like(rho)
        for q in range(19):
            if LATTICE[q, axis_c] != 0:
                moment = moment + float(LATTICE[q, axis_c]) * pops[q]
        moments.append(moment)
    velocity = [(moments[a] + 0.5 * force[a]) / rho for a in range(3)]
    usq = velocity[0] * velocity[0] + velocity[1] * velocity[1] + velocity[2] * velocity[2]
    udotf = velocity[0] * force[0] + velocity[1] * force[1] + velocity[2] * force[2]
    posts = []
    for q in range(19):
        cu = jnp.zeros_like(rho)
        cf = jnp.zeros_like(rho)
        for a in range(3):
            if LATTICE[q, a] != 0:
                cu = cu + float(LATTICE[q, a]) * velocity[a]
                cf = cf + float(LATTICE[q, a]) * force[a]
        weight = LATTICE_WEIGHTS[q]
        feq = weight * rho * (1.0 + 3.0 * cu + 4.5 * cu * cu - 1.5 * usq)
        source = weight * (1.0 - 0.5 / RELAX) * (3.0 * (cf - udotf) + 9.0 * cu * cf)
        posts.append(pops[q] - (pops[q] - feq) / RELAX + source)
    return posts, jnp.stack(velocity)


def reference(populations, displacement, offsets, cell_local, destination, triangles, stiffness):
    owner = (jnp.arange(TRIS, dtype=jnp.int32) // TRI_DEV) * M_DEV
    vertices = triangles + owner[:, None]
    marker_force = membrane_force(displacement, vertices, stiffness, MARKERS)
    tile = destination[:, 0]
    global_x = (tile // N_GY) * CX + cell_local[0]
    global_y = (tile % N_GY) * CY + cell_local[1]
    cell_flat = (global_x * NY + global_y) * CZ + cell_local[2]
    indices, weights = corner_terms(offsets, cell_flat, NY * CZ, CZ)
    values = (marker_force[:, None, :] * weights[None]).reshape(3, -1)
    body_force = jnp.zeros((3, NX * NY * CZ), jnp.float32).at[:, indices.reshape(-1)].add(values)
    body_force = body_force.reshape(3, NX, NY, CZ)
    posts, velocity = collide(populations, body_force)
    moved = []
    for q in range(19):
        moved.append(jnp.roll(posts[q], (int(LATTICE[q, 0]), int(LATTICE[q, 1]), int(LATTICE[q, 2])), axis=(0, 1, 2)))
    populations_next = jnp.stack(moved)
    flat_velocity = velocity.reshape(3, -1)
    marker_velocity = jnp.sum(flat_velocity[:, indices] * weights[None], axis=1)
    return populations_next, marker_velocity
```

```python
import jax
import jax.numpy as jnp
import numpy as np
from jax import lax
from jax.experimental import pallas as pl
from jax.experimental.pallas import tpu as pltpu
from jax.sharding import PartitionSpec as P

CAP = 128
LANES = 128
WINDOW = 32

LATTICE = np.array(
    [
        [0, 0, 0],
        [1, 0, 0],
        [-1, 0, 0],
        [0, 1, 0],
        [0, -1, 0],
        [0, 0, 1],
        [0, 0, -1],
        [1, 1, 0],
        [-1, -1, 0],
        [1, -1, 0],
        [-1, 1, 0],
        [1, 0, 1],
        [-1, 0, -1],
        [1, 0, -1],
        [-1, 0, 1],
        [0, 1, 1],
        [0, -1, -1],
        [0, 1, -1],
        [0, -1, 1],
    ]
)
LATTICE_WEIGHTS = [1.0 / 3.0] + [1.0 / 18.0] * 6 + [1.0 / 36.0] * 12
RELAX = 0.8
X_PLUS = [q for q in range(19) if LATTICE[q, 0] == 1]
X_MINUS = [q for q in range(19) if LATTICE[q, 0] == -1]
Y_PLUS = [q for q in range(19) if LATTICE[q, 1] == 1]
Y_MINUS = [q for q in range(19) if LATTICE[q, 1] == -1]
DIAGONAL = [q for q in range(19) if LATTICE[q, 0] != 0 and LATTICE[q, 1] != 0]
NT = (((1,), (1,)), ((), ()))
F32 = jnp.float32
BF16 = jnp.bfloat16
I32 = jnp.int32
MIB = 1 << 20


def iota(shape, dim):
    return lax.broadcasted_iota(I32, shape, dim)


def split(value):
    high = value.astype(BF16)
    low = (value - high.astype(F32)).astype(BF16)
    return high, low


def one_hot(hit):
    return jnp.where(hit, 1.0, 0.0).astype(BF16)


def lane_pick(row, lanes):
    return jnp.take_along_axis(jnp.broadcast_to(row, lanes.shape), lanes, axis=1)


def sender_kernel(
    disp_ref,
    offs_ref,
    cell_ref,
    dest_ref,
    tri_ref,
    stiff_ref,
    packed_ref,
    slot_ref,
    disp_rows,
    pay,
    tri_rows,
    term_high,
    term_low,
    acc,
    mask,
    before,
    codes,
    slots_hot,
    inverse,
):
    count = disp_ref.shape[1]
    rows = count // LANES
    tri_rows_count = tri_ref.shape[1] // LANES
    tiles = packed_ref.shape[1]
    for r in range(rows):
        lane = pl.ds(r * LANES, LANES)
        flat = (cell_ref[0:1, lane] * 32 + cell_ref[1:2, lane]) * 256 + cell_ref[2:3, lane]
        pay[6, r : r + 1, :] = flat.astype(F32)
        for c in range(3):
            disp_rows[c, r : r + 1, :] = disp_ref[c : c + 1, lane]
            pay[3 + c, r : r + 1, :] = offs_ref[c : c + 1, lane]
    for r in range(tri_rows_count):
        for v in range(3):
            tri_rows[v, r : r + 1, :] = tri_ref[v : v + 1, pl.ds(r * LANES, LANES)]

    def gather_step(i, carry):
        block = pl.ds(pl.multiple_of(i * 8, 8), 8)
        corner = []
        for v in range(3):
            index = tri_rows[v, block, :]
            low = index & (LANES - 1)
            high = index >> 7
            found = [jnp.zeros((8, LANES), F32) for _ in range(3)]
            for r in range(rows):
                hit = high == r
                for c in range(3):
                    found[c] = jnp.where(hit, lane_pick(disp_rows[c, r : r + 1, :], low), found[c])
            corner.append(found)
        stiff = stiff_ref[block, :]
        for c in range(3):
            total = corner[0][c] + corner[1][c] + corner[2][c]
            for v in range(3):
                term = stiff * (total - 3.0 * corner[v][c])
                rounded = term.astype(BF16).astype(F32)
                term_high[v, c, block, :] = rounded
                term_low[v, c, block, :] = term - rounded
        return carry

    lax.fori_loop(0, tri_rows_count // 8, gather_step, 0)

    acc[...] = jnp.zeros_like(acc)
    row_iota = iota((rows, LANES), 0)
    lane_iota = iota((LANES, LANES), 0)
    for v in range(3):

        def scatter_step(i, carry, v=v):
            left = []
            right = []
            for k in range(8):
                at = pl.ds(i * 8 + k, 1)
                index = tri_rows[v, at, :]
                hit = row_iota == (index >> 7)
                parts = []
                for c in range(3):
                    parts.append(jnp.where(hit, term_high[v, c, at, :], 0.0).astype(BF16))
                    parts.append(jnp.where(hit, term_low[v, c, at, :], 0.0).astype(BF16))
                left.append(jnp.concatenate(parts, axis=0))
                right.append(one_hot(lane_iota == (index & (LANES - 1))))
            acc[...] += lax.dot_general(
                jnp.concatenate(left, axis=1),
                jnp.concatenate(right, axis=1),
                NT,
                preferred_element_type=F32,
            )
            return carry

        lax.fori_loop(0, tri_rows_count // 8, scatter_step, 0)
    for c in range(3):
        at = c * 2 * rows
        pay[c] = acc[at : at + rows, :] + acc[at + rows : at + 2 * rows, :]

    width = 256
    blocks = count // width
    tile_iota = iota((tiles, width), 0)
    earlier = one_hot(iota((width, 2 * width), 0) < iota((width, 2 * width), 1))
    for b in range(blocks):
        lane = pl.ds(b * width, width)
        hit = one_hot(dest_ref[0:1, lane] == tile_iota)
        mask[:, lane] = hit
        before[b] = jnp.dot(hit, earlier, preferred_element_type=F32)
    running = jnp.zeros((tiles, width), F32)
    within = iota((1, width), 1).astype(F32)
    for b in range(blocks):
        lane = pl.ds(b * width, width)
        hit = dest_ref[0:1, lane] == tile_iota
        own = before[b, :, 0:width] + running
        slot = jnp.sum(jnp.where(hit, own, 0.0), axis=0, keepdims=True)
        running = running + before[b, :, width:]
        slot = slot.astype(I32)
        slot_ref[0:1, lane] = slot
        slots_hot[:, lane] = one_hot(slot == iota((CAP, width), 0))
        codes[0:tiles, lane] = jnp.where(hit, within, 0.0).astype(BF16)
        codes[tiles : 2 * tiles, lane] = jnp.where(hit, float(b + 1), 0.0).astype(BF16)
    inverse[...] = lax.dot_general(codes[...], slots_hot[...], NT, preferred_element_type=F32)

    def pack_step(i, carry):
        at = pl.multiple_of(i * 8, 8)
        block = pl.ds(at, 8)
        group = inverse[pl.ds(pl.multiple_of(tiles + i * 8, 8), 8), :]
        valid = group > 0.5
        marker = ((group - 1.0) * float(width) + inverse[block, :]).astype(I32)
        marker = jnp.maximum(marker, 0)
        low = marker & (LANES - 1)
        high = marker >> 7
        found = [jnp.zeros((8, LANES), F32) for _ in range(7)]
        for r in range(rows):
            hit = high == r
            for c in range(7):
                found[c] = jnp.where(hit, lane_pick(pay[c, r : r + 1, :], low), found[c])
        for c in range(7):
            packed_ref[c, block, :] = jnp.where(valid, found[c], -1.0 if c == 6 else 0.0)
        return carry

    lax.fori_loop(0, tiles // 8, pack_step, 0)


def sender(displacement, offsets, cell_local, destination, triangles, stiffness, tiles):
    count = displacement.shape[1]
    tris = triangles.shape[1]
    rows = count // LANES
    return pl.pallas_call(
        sender_kernel,
        out_shape=(
            jax.ShapeDtypeStruct((7, tiles, CAP), F32),
            jax.ShapeDtypeStruct((1, count), I32),
        ),
        in_specs=[pl.BlockSpec(memory_space=pltpu.VMEM)] * 6,
        out_specs=(pl.BlockSpec(memory_space=pltpu.VMEM),) * 2,
        scratch_shapes=[
            pltpu.VMEM((3, rows, LANES), F32),
            pltpu.VMEM((7, rows, LANES), F32),
            pltpu.VMEM((3, tris // LANES, LANES), I32),
            pltpu.VMEM((3, 3, tris // LANES, LANES), F32),
            pltpu.VMEM((3, 3, tris // LANES, LANES), F32),
            pltpu.VMEM((6 * rows, LANES), F32),
            pltpu.VMEM((tiles, count), BF16),
            pltpu.VMEM((count // 256, tiles, 512), F32),
            pltpu.VMEM((2 * tiles, count), BF16),
            pltpu.VMEM((CAP, count), BF16),
            pltpu.VMEM((2 * tiles, CAP), F32),
        ],
        compiler_params=pltpu.CompilerParams(vmem_limit_bytes=40 * MIB),
        name="sender",
    )(displacement, offsets, cell_local, destination, triangles, stiffness)


def chunk_rows(arrived, i):
    out = []
    for c in range(7):
        out.append(
            jnp.concatenate(
                [arrived[c, pl.ds(2 * i, 1), :], arrived[c, pl.ds(2 * i + 1, 1), :]], axis=1
            )
        )
    return out


def plane_weights(rows):
    cell = rows[6].astype(I32)
    y = (cell >> 8) & 31
    x = cell >> 13
    eight = iota((8, 2 * LANES), 0)
    weight_x = jnp.where(
        eight == x, 1.0 - rows[3], jnp.where(eight == x + 1, rows[3], 0.0)
    )

    def weight_y(at):
        return jnp.where(y == at, 1.0 - rows[4], jnp.where(y + 1 == at, rows[4], 0.0))

    return weight_x, weight_y


def fluid_kernel(
    arrived_ref,
    pops_ref,
    force_ref,
    vel_ref,
    arrived,
    pops,
    field,
    depth_high,
    depth_low,
    vel_high,
    vel_low,
    vel_rows,
    pops_sem,
):
    fetch = pltpu.make_async_copy(pops_ref, pops, pops_sem)
    fetch.start()
    chunks = CAP // 2
    wide = 2 * LANES
    cells_x, cells_y, cells_z = force_ref.shape[1:]
    for c in range(7):
        arrived[c] = arrived_ref[c].T
    field[...] = jnp.zeros_like(field)
    depth_iota = iota((cells_z, wide), 0)
    span = WINDOW * 24

    def spread_step(i, carry):
        rows = chunk_rows(arrived, i)
        depth = rows[6].astype(I32) & 255
        first = depth_iota == depth
        second = depth_iota == depth + 1
        lower = 1.0 - rows[5]
        lower_high = lower.astype(BF16).astype(F32)
        upper_high = rows[5].astype(BF16).astype(F32)
        high = jnp.where(first, lower_high, jnp.where(second, upper_high, 0.0)).astype(BF16)
        low = jnp.where(
            first, lower - lower_high, jnp.where(second, rows[5] - upper_high, 0.0)
        ).astype(BF16)
        depth_high[i] = high
        depth_low[i] = low
        weight_x, weight_y = plane_weights(rows)
        pushed = [weight_x * rows[c] for c in range(3)]
        parts = []
        for y in range(WINDOW):
            at_y = weight_y(y)
            for c in range(3):
                parts.append(pushed[c] * at_y)
        spread_high, spread_low = split(jnp.concatenate(parts, axis=0))
        both = lax.dot_general(
            jnp.concatenate([spread_high, spread_low], axis=0),
            high,
            NT,
            preferred_element_type=F32,
        )
        third = lax.dot_general(spread_high, low, NT, preferred_element_type=F32)
        add = both[0:span] + both[span:] + third
        field[0, 0:span, :] += add[:, 0:LANES]
        field[1, 0:span, :] += add[:, LANES:]
        return carry

    lax.fori_loop(0, chunks, spread_step, 0)

    fetch.wait()

    def velocity_step(x, carry):
        rho = pops[0, x]
        for q in range(1, 19):
            rho = rho + pops[q, x]
        inverse = 1.0 / rho
        for c in range(3):
            moment = None
            for q in range(19):
                if LATTICE[q, c] != 0:
                    value = pops[q, x]
                    if moment is None:
                        moment = value if LATTICE[q, c] > 0 else -value
                    else:
                        moment = moment + value if LATTICE[q, c] > 0 else moment - value
            at = pl.ds(c * 8 + x, cells_y, stride=24)
            for half in range(2):
                lane = slice(half * LANES, half * LANES + LANES)
                pull = field[half, at, :]
                force_ref[c, x, :, lane] = pull
                field[half, at, :] = (moment[:, lane] + 0.5 * pull) * inverse[:, lane]
        return carry

    for x in range(cells_x):
        velocity_step(x, 0)
    for half in range(2):
        lane = slice(half * LANES, half * LANES + LANES)
        vel_high[:, lane], vel_low[:, lane] = split(field[half])

    def gather_step(i, carry):
        rows = chunk_rows(arrived, i)
        weight_x, weight_y = plane_weights(rows)
        upper = vel_high[0:span, :]
        both = jnp.dot(
            jnp.concatenate([upper, vel_low[0:span, :]], axis=0),
            depth_high[i],
            preferred_element_type=F32,
        )
        third = jnp.dot(upper, depth_low[i], preferred_element_type=F32)
        total = both[0:span] + both[span:] + third
        sums = [jnp.zeros((8, wide), F32) for _ in range(3)]
        for y in range(WINDOW):
            plane = weight_x * weight_y(y)
            for c in range(3):
                at = y * 24 + c * 8
                sums[c] = sums[c] + plane * total[at : at + 8]
        for c in range(3):
            value = jnp.sum(sums[c], axis=0, keepdims=True)
            vel_rows[c, pl.ds(2 * i, 1), :] = value[:, 0:LANES]
            vel_rows[c, pl.ds(2 * i + 1, 1), :] = value[:, LANES:]
        return carry

    lax.fori_loop(0, chunks, gather_step, 0)
    for c in range(3):
        vel_ref[c] = vel_rows[c].T


def fluid(arrived, populations):
    shape = populations.shape
    sources = arrived.shape[1]
    lines = shape[2] * 24
    return pl.pallas_call(
        fluid_kernel,
        out_shape=(
            jax.ShapeDtypeStruct((3,) + shape[1:], F32),
            jax.ShapeDtypeStruct((3, sources, CAP), F32),
        ),
        in_specs=[
            pl.BlockSpec(memory_space=pltpu.VMEM),
            pl.BlockSpec(memory_space=pl.ANY),
        ],
        out_specs=(pl.BlockSpec(memory_space=pltpu.VMEM),) * 2,
        scratch_shapes=[
            pltpu.VMEM((7, CAP, sources), F32),
            pltpu.VMEM(shape, F32),
            pltpu.VMEM((2, lines, LANES), F32),
            pltpu.VMEM((CAP // 2, shape[3], 2 * LANES), BF16),
            pltpu.VMEM((CAP // 2, shape[3], 2 * LANES), BF16),
            pltpu.VMEM((lines, shape[3]), BF16),
            pltpu.VMEM((lines, shape[3]), BF16),
            pltpu.VMEM((3, CAP, sources), F32),
            pltpu.SemaphoreType.DMA,
        ],
        compiler_params=pltpu.CompilerParams(vmem_limit_bytes=50 * MIB),
        name="fluid",
    )(arrived, populations)


def collide_kernel(pops, force, moved, x_plus, x_minus, y_plus, y_minus, pp, mm, pm, mp):
    cells_x, cells_y = force.shape[1:3]

    def plane(x, carry):
        rho = pops[0, x]
        for q in range(1, 19):
            rho = rho + pops[q, x]
        inverse = 1.0 / rho
        pull = [force[c, x] for c in range(3)]
        velocity = []
        for c in range(3):
            moment = None
            for q in range(19):
                if LATTICE[q, c] != 0:
                    value = pops[q, x]
                    if moment is None:
                        moment = value if LATTICE[q, c] > 0 else -value
                    else:
                        moment = moment + value if LATTICE[q, c] > 0 else moment - value
            velocity.append((moment + 0.5 * pull[c]) * inverse)
        usq = velocity[0] * velocity[0] + velocity[1] * velocity[1] + velocity[2] * velocity[2]
        udotf = velocity[0] * pull[0] + velocity[1] * pull[1] + velocity[2] * pull[2]
        push = 1.0 - 0.5 / RELAX
        base = rho * (1.0 - 1.5 * usq) * (1.0 / RELAX) - (3.0 * push) * udotf
        rest = 1.0 - 1.0 / RELAX

        def terms(q):
            along = None
            pulled = None
            for c in range(3):
                if LATTICE[q, c] != 0:
                    u = velocity[c] if LATTICE[q, c] > 0 else -velocity[c]
                    f = pull[c] if LATTICE[q, c] > 0 else -pull[c]
                    along = u if along is None else along + u
                    pulled = f if pulled is None else pulled + f
            return along, pulled

        def emit(q, value):
            weight_value = value
            cx, cy, cz = (int(v) for v in LATTICE[q])
            if cy != 0:
                weight_value = pltpu.roll(weight_value, cy % cells_y, 0)
            if cz != 0:
                weight_value = pltpu.roll(weight_value, cz % weight_value.shape[1], 1)
            to = x + cx
            if cx > 0:
                to = jnp.where(to == cells_x, 0, to)
            if cx < 0:
                to = jnp.where(to < 0, cells_x - 1, to)
            moved[q, to] = weight_value

        emit(0, rest * pops[0, x] + LATTICE_WEIGHTS[0] * base)
        for q in range(1, 19, 2):
            along, pulled = terms(q)
            odd = (3.0 / RELAX) * rho * along + (3.0 * push) * pulled
            even = base + along * ((4.5 / RELAX) * rho * along + (9.0 * push) * pulled)
            weight = LATTICE_WEIGHTS[q]
            emit(q, rest * pops[q, x] + weight * (even + odd))
            emit(q + 1, rest * pops[q + 1, x] + weight * (even - odd))
        return carry

    lax.fori_loop(0, cells_x, plane, 0)
    last_x = cells_x - 1
    last_y = cells_y - 1
    for n in range(5):
        x_plus[n] = moved[X_PLUS[n], 0]
        x_minus[n] = moved[X_MINUS[n], last_x]
        for x in range(cells_x):
            y_plus[n, x : x + 1, :] = moved[Y_PLUS[n], x, 0:1, :]
            y_minus[n, x : x + 1, :] = moved[Y_MINUS[n], x, last_y:, :]
    pp[...] = moved[7, 0, 0:1, :]
    mm[...] = moved[8, last_x, last_y:, :]
    pm[...] = moved[9, 0, last_y:, :]
    mp[...] = moved[10, last_x, 0:1, :]


def collide(populations, force):
    _, cells_x, cells_y, cells_z = populations.shape
    face_x = jax.ShapeDtypeStruct((5, cells_y, cells_z), F32)
    face_y = jax.ShapeDtypeStruct((5, cells_x, cells_z), F32)
    line = jax.ShapeDtypeStruct((1, cells_z), F32)
    return pl.pallas_call(
        collide_kernel,
        out_shape=(
            jax.ShapeDtypeStruct(populations.shape, F32),
            face_x,
            face_x,
            face_y,
            face_y,
            line,
            line,
            line,
            line,
        ),
        in_specs=[pl.BlockSpec(memory_space=pltpu.VMEM)] * 2,
        out_specs=(pl.BlockSpec(memory_space=pltpu.VMEM),) * 9,
        compiler_params=pltpu.CompilerParams(vmem_limit_bytes=50 * MIB),
        cost_estimate=pl.CostEstimate(
            flops=400 * cells_x * cells_y * cells_z,
            bytes_accessed=4 * 45 * cells_x * cells_y * cells_z,
            transcendentals=0,
        ),
        name="collide",
    )(populations, force)


def patch_kernel(
    moved, x_plus, x_minus, y_plus, y_minus, pp, mm, pm, mp, out, blocks, read_sem, write_sem
):
    cells_x, cells_y = out.shape[1:3]
    corners = {7: pp, 8: mm, 9: pm, 10: mp}
    reads = []
    for n, q in enumerate(Y_PLUS + Y_MINUS):
        at = 0 if n < 5 else cells_y - 8
        reads.append(
            pltpu.make_async_copy(out.at[q, :, pl.ds(at, 8), :], blocks.at[n], read_sem.at[n])
        )
        reads[-1].start()
    writes = []

    def send(source, target):
        copy = pltpu.make_async_copy(source, target, write_sem.at[len(writes)])
        copy.start()
        writes.append(copy)

    for faces, qs, x in ((x_plus, X_PLUS, 0), (x_minus, X_MINUS, cells_x - 1)):
        for n, q in enumerate(qs):
            if LATTICE[q, 1] == 0:
                send(faces.at[n], out.at[q, x])
            else:
                at = 8 if LATTICE[q, 1] > 0 else 0
                rest = pl.ds(at, cells_y - 8)
                send(faces.at[n, rest, :], out.at[q, x, rest, :])
    for n, q in enumerate(Y_PLUS + Y_MINUS):
        reads[n].wait()
        faces, row = (y_plus, 0) if n < 5 else (y_minus, 7)
        at = 0 if n < 5 else cells_y - 8
        wall = None
        if q in DIAGONAL:
            wall = 0 if LATTICE[q, 0] > 0 else cells_x - 1
            source, qs = (x_plus, X_PLUS) if LATTICE[q, 0] > 0 else (x_minus, X_MINUS)
            blocks[n, wall] = source[qs.index(q), at : at + 8, :]
        for x in range(cells_x):
            if x == wall:
                blocks[n, x, row : row + 1, :] = corners[q][...]
            else:
                blocks[n, x, row : row + 1, :] = faces[n % 5, x : x + 1, :]
        send(blocks.at[n], out.at[q, :, pl.ds(at, 8), :])
    for copy in writes:
        copy.wait()


def patch(moved, halos):
    _, cells_x, cells_y, cells_z = moved.shape
    return pl.pallas_call(
        patch_kernel,
        out_shape=jax.ShapeDtypeStruct(moved.shape, F32),
        in_specs=[pl.BlockSpec(memory_space=pl.ANY)] + [pl.BlockSpec(memory_space=pltpu.VMEM)] * 8,
        out_specs=pl.BlockSpec(memory_space=pl.ANY),
        scratch_shapes=[
            pltpu.VMEM((10, cells_x, 8, cells_z), F32),
            pltpu.SemaphoreType.DMA((10,)),
            pltpu.SemaphoreType.DMA((20,)),
        ],
        input_output_aliases={0: 0},
        compiler_params=pltpu.CompilerParams(vmem_limit_bytes=32 * MIB),
        cost_estimate=pl.CostEstimate(
            flops=0, bytes_accessed=4 * 20 * cells_x * 32 * cells_z, transcendentals=0
        ),
        name="patch",
    )(moved, *halos)


def unpack_kernel(returned, dest_ref, slot_ref, out_ref):
    tiles = returned.shape[1]
    blocks = dest_ref.shape[0] // 8
    for i in range(blocks):
        dest = dest_ref[8 * i : 8 * i + 8, :]
        slot = slot_ref[8 * i : 8 * i + 8, :]

        def pick_step(g, found, dest=dest, slot=slot):
            found = list(found)
            for j in range(8):
                k = g * 8 + j
                hit = dest == k
                for c in range(3):
                    value = lane_pick(returned[c, pl.ds(k, 1), :], slot)
                    found[c] = jnp.where(hit, value, found[c])
            return tuple(found)

        zero = jnp.zeros((8, LANES), F32)
        found = lax.fori_loop(0, tiles // 8, pick_step, (zero, zero, zero))
        for c in range(3):
            for r in range(8):
                at = (8 * i + r) * LANES
                out_ref[c : c + 1, at : at + LANES] = found[c][r : r + 1, :]


def unpack(returned, dest, slot):
    count = dest.size
    return pl.pallas_call(
        unpack_kernel,
        out_shape=jax.ShapeDtypeStruct((3, count), F32),
        in_specs=[pl.BlockSpec(memory_space=pltpu.VMEM)] * 3,
        out_specs=pl.BlockSpec(memory_space=pltpu.VMEM),
        compiler_params=pltpu.CompilerParams(vmem_limit_bytes=32 * MIB),
        name="unpack",
    )(returned, dest, slot)


def exchange(faces):
    size_x = lax.axis_size("gx")
    size_y = lax.axis_size("gy")

    def along(axis, size, step):
        perm = [(i, (i + step) % size) for i in range(size)]
        return lambda value: lax.ppermute(value, axis, perm)

    def across(step_x, step_y):
        perm = []
        for i in range(size_x):
            for j in range(size_y):
                target = ((i + step_x) % size_x) * size_y + (j + step_y) % size_y
                perm.append((i * size_y + j, target))
        return lambda value: lax.ppermute(value, ("gx", "gy"), perm)

    routes = [
        along("gx", size_x, 1),
        along("gx", size_x, -1),
        along("gy", size_y, 1),
        along("gy", size_y, -1),
        across(1, 1),
        across(-1, -1),
        across(1, -1),
        across(-1, 1),
    ]
    return [route(face) for route, face in zip(routes, faces)]


def shards(populations, displacement, offsets, cell_local, destination, triangles, stiffness):
    tiles = lax.axis_size("gx") * lax.axis_size("gy")
    count = displacement.shape[1]
    packed, slot = sender(
        displacement,
        offsets,
        cell_local,
        destination.reshape(1, count),
        triangles.T,
        stiffness.reshape(-1, LANES),
        tiles,
    )
    arrived = lax.all_to_all(packed, ("gx", "gy"), split_axis=1, concat_axis=1, tiled=True)
    force, slot_velocity = fluid(arrived, populations)
    returned = lax.all_to_all(slot_velocity, ("gx", "gy"), split_axis=1, concat_axis=1, tiled=True)
    moved, *faces = collide(populations, force)
    populations_next = patch(moved, exchange(faces))
    marker_velocity = unpack(
        returned, destination.reshape(-1, LANES), slot.reshape(-1, LANES)
    )
    return (populations_next, marker_velocity)


def solution(mesh):
    return jax.shard_map(
        shards,
        mesh=mesh,
        in_specs=(
            P(None, "gx", "gy", None),
            P(None, ("gx", "gy")),
            P(None, ("gx", "gy")),
            P(None, ("gx", "gy")),
            P(("gx", "gy"), None),
            P(("gx", "gy"), None),
            P(("gx", "gy")),
        ),
        out_specs=(P(None, "gx", "gy", None), P(None, ("gx", "gy"))),
        check_vma=False,
    )
```

```python
import jax
import jax.numpy as jnp
import numpy as np
from jax import lax
from jax.experimental import pallas as pl
from jax.experimental.pallas import tpu as pltpu
from jax.sharding import PartitionSpec as P

CAP = 128
LANES = 128
WINDOW = 12
RANKS = 8
WIDE = RANKS * LANES

LATTICE = np.array(
    [
        [0, 0, 0],
        [1, 0, 0],
        [-1, 0, 0],
        [0, 1, 0],
        [0, -1, 0],
        [0, 0, 1],
        [0, 0, -1],
        [1, 1, 0],
        [-1, -1, 0],
        [1, -1, 0],
        [-1, 1, 0],
        [1, 0, 1],
        [-1, 0, -1],
        [1, 0, -1],
        [-1, 0, 1],
        [0, 1, 1],
        [0, -1, -1],
        [0, 1, -1],
        [0, -1, 1],
    ]
)
LATTICE_WEIGHTS = [1.0 / 3.0] + [1.0 / 18.0] * 6 + [1.0 / 36.0] * 12
RELAX = 0.8
X_PLUS = [q for q in range(19) if LATTICE[q, 0] == 1]
X_MINUS = [q for q in range(19) if LATTICE[q, 0] == -1]
Y_PLUS = [q for q in range(19) if LATTICE[q, 1] == 1]
Y_MINUS = [q for q in range(19) if LATTICE[q, 1] == -1]
DIAGONAL = [q for q in range(19) if LATTICE[q, 0] != 0 and LATTICE[q, 1] != 0]
NT = (((1,), (1,)), ((), ()))
F32 = jnp.float32
BF16 = jnp.bfloat16
I32 = jnp.int32
MIB = 1 << 20


def iota(shape, dim):
    return lax.broadcasted_iota(I32, shape, dim)


def split(value):
    high = value.astype(BF16)
    low = (value - high.astype(F32)).astype(BF16)
    return high, low


def one_hot(hit):
    return jnp.where(hit, 1.0, 0.0).astype(BF16)


def lane_pick(row, lanes):
    return jnp.take_along_axis(jnp.broadcast_to(row, lanes.shape), lanes, axis=1)


def sender_kernel(
    disp_hbm,
    offs_hbm,
    cell_hbm,
    dest_hbm,
    tri_hbm,
    stiff_hbm,
    packed_ref,
    slot_ref,
    disp_ref,
    offs_ref,
    cell_ref,
    dest_ref,
    tri_ref,
    stiff_ref,
    disp_rows,
    pay,
    tri_rows,
    term_high,
    term_low,
    acc,
    order,
    place,
    sorted_dest,
    sorted_slot,
    mask,
    sems,
):
    fetches = []
    for n, (source, target) in enumerate(
        (
            (cell_hbm, cell_ref),
            (dest_hbm, dest_ref),
            (tri_hbm, tri_ref),
            (disp_hbm, disp_ref),
            (stiff_hbm, stiff_ref),
            (offs_hbm, offs_ref),
        )
    ):
        fetches.append(pltpu.make_async_copy(source, target, sems.at[n]))
        fetches[-1].start()
    count = disp_ref.shape[1]
    rows = count // LANES
    tri_rows_count = tri_ref.shape[1] // LANES
    tiles = packed_ref.shape[1]
    width = 256
    blocks = count // width
    bins = 32
    for fetch in fetches:
        fetch.wait()
    for r in range(rows):
        lane = pl.ds(r * LANES, LANES)
        flat = (cell_ref[0:1, lane] * 32 + cell_ref[1:2, lane]) * 256 + cell_ref[2:3, lane]
        pay[6, r : r + 1, :] = flat.astype(F32)
        for c in range(3):
            disp_rows[c, r : r + 1, :] = disp_ref[c : c + 1, lane]
            pay[3 + c, r : r + 1, :] = offs_ref[c : c + 1, lane]
    for r in range(tri_rows_count):
        for v in range(3):
            tri_rows[v, r : r + 1, :] = tri_ref[v : v + 1, pl.ds(r * LANES, LANES)]

    earlier = one_hot(iota((width, 2 * width), 0) < iota((width, 2 * width), 1))
    bin_iota = iota((bins, width), 0)
    y_hits = [cell_ref[1:2, b * width : (b + 1) * width] == bin_iota for b in range(blocks)]
    y_counts = jnp.dot(
        jnp.concatenate([one_hot(hit) for hit in y_hits], axis=0),
        earlier,
        preferred_element_type=F32,
    )
    totals = y_counts[0:bins, width:]
    for b in range(1, blocks):
        totals = totals + y_counts[b * bins : (b + 1) * bins, width:]
    below = jnp.where(iota((bins, bins), 1) < iota((bins, bins), 0), 1.0, 0.0)
    first = jnp.dot(below, totals, preferred_element_type=F32, precision=lax.Precision.HIGHEST)
    within = iota((1, width), 1).astype(F32)
    running = first
    left = []
    right = []
    for b in range(blocks):
        own = y_counts[b * bins : (b + 1) * bins, 0:width] + running
        running = running + y_counts[b * bins : (b + 1) * bins, width:]
        at = jnp.sum(jnp.where(y_hits[b], own, 0.0), axis=0, keepdims=True).astype(I32)
        place[2 * b : 2 * b + 1, :] = at[:, 0:LANES]
        place[2 * b + 1 : 2 * b + 2, :] = at[:, LANES:]
        hit = (at >> 7) == iota((rows, width), 0)
        left.append(
            jnp.concatenate(
                [
                    jnp.where(hit, within, 0.0).astype(BF16),
                    jnp.where(hit, float(b), 0.0).astype(BF16),
                ],
                axis=0,
            )
        )
        right.append(one_hot((at & (LANES - 1)) == iota((LANES, width), 0)))
    order[...] = lax.dot_general(
        jnp.concatenate(left, axis=1),
        jnp.concatenate(right, axis=1),
        NT,
        preferred_element_type=F32,
    )
    for i in range(rows // 8):
        block = slice(8 * i, 8 * i + 8)
        marker = (order[rows + 8 * i : rows + 8 * i + 8, :] * 256.0 + order[block, :]).astype(I32)
        low = marker & (LANES - 1)
        high = marker >> 7
        found = jnp.zeros((8, LANES), I32)
        for r in range(rows):
            found = jnp.where(high == r, lane_pick(dest_ref[r : r + 1, :], low), found)
        sorted_dest[block, :] = found

    def row_of(ref, b, at=0):
        return jnp.concatenate(
            [ref[at + 2 * b : at + 2 * b + 1, :], ref[at + 2 * b + 1 : at + 2 * b + 2, :]], axis=1
        )

    tile_iota = iota((tiles, width), 0)
    hots = []
    cums = []
    for b in range(blocks):
        mask[:, b * width : (b + 1) * width] = one_hot(row_of(sorted_dest, b) == tile_iota)
        at = within + float(b * width)
        hots.append((at >= first) & (at < first + totals))
        cums.append(one_hot(at < first))
    before = jnp.dot(
        jnp.concatenate([mask[:, b * width : (b + 1) * width] for b in range(blocks)], axis=0),
        earlier,
        preferred_element_type=F32,
    )
    smaller = lax.dot_general(
        jnp.concatenate(cums, axis=1), mask[...], NT, preferred_element_type=F32
    )
    room = float(CAP) - smaller[bins - 1 : bins, :]
    ahead = jnp.zeros((1, tiles), F32)
    shift = []
    for y in range(bins):
        ahead = jnp.maximum(ahead, float((y * CAP) // (bins - 1)) - smaller[y : y + 1, :])
        shift.append(jnp.minimum(ahead, room))
    shift = jnp.concatenate(shift, axis=0).astype(BF16)
    shifts = jnp.dot(shift, mask[...], preferred_element_type=F32)
    running = jnp.zeros((tiles, width), F32)
    left = []
    right = []
    for b in range(blocks):
        lane = slice(b * width, (b + 1) * width)
        hit = row_of(sorted_dest, b) == tile_iota
        own = before[b * tiles : (b + 1) * tiles, 0:width] + running
        running = running + before[b * tiles : (b + 1) * tiles, width:]
        slot = jnp.sum(jnp.where(hit, own, 0.0), axis=0, keepdims=True) + jnp.sum(
            jnp.where(hots[b], shifts[:, lane], 0.0), axis=0, keepdims=True
        )
        slot = slot.astype(I32)
        sorted_slot[2 * b : 2 * b + 1, :] = slot[:, 0:LANES]
        sorted_slot[2 * b + 1 : 2 * b + 2, :] = slot[:, LANES:]
        left.append(
            jnp.concatenate(
                [
                    jnp.where(hit, row_of(order, b), 0.0).astype(BF16),
                    jnp.where(hit, row_of(order, b, rows) + 1.0, 0.0).astype(BF16),
                ],
                axis=0,
            )
        )
        right.append(one_hot(slot == iota((CAP, width), 0)))
    inverse = lax.dot_general(
        jnp.concatenate(left, axis=1),
        jnp.concatenate(right, axis=1),
        NT,
        preferred_element_type=F32,
    )
    for i in range(rows // 8):
        block = slice(8 * i, 8 * i + 8)
        at = place[block, :]
        low = at & (LANES - 1)
        high = at >> 7
        found = jnp.zeros((8, LANES), I32)
        for r in range(rows):
            found = jnp.where(high == r, lane_pick(sorted_slot[r : r + 1, :], low), found)
        slot_ref[block, :] = found

    def gather_step(i, carry):
        block = pl.ds(pl.multiple_of(i * 8, 8), 8)
        corner = []
        for v in range(3):
            index = tri_rows[v, block, :]
            low = index & (LANES - 1)
            high = index >> 7
            found = [jnp.zeros((8, LANES), F32) for _ in range(3)]
            for r in range(rows):
                hit = high == r
                for c in range(3):
                    found[c] = jnp.where(hit, lane_pick(disp_rows[c, r : r + 1, :], low), found[c])
            corner.append(found)
        stiff = stiff_ref[block, :]
        for c in range(3):
            total = corner[0][c] + corner[1][c] + corner[2][c]
            for v in range(3):
                term = stiff * (total - 3.0 * corner[v][c])
                rounded = term.astype(BF16).astype(F32)
                term_high[v, c, block, :] = rounded
                term_low[v, c, block, :] = term - rounded
        return carry

    lax.fori_loop(0, tri_rows_count // 8, gather_step, 0)

    acc[...] = jnp.zeros_like(acc)
    row_iota = iota((rows, LANES), 0)
    lane_iota = iota((LANES, LANES), 0)
    step_rows = 32
    for v in range(3):

        def scatter_step(i, carry, v=v):
            left = []
            right = []
            for k in range(step_rows):
                at = pl.ds(i * step_rows + k, 1)
                index = tri_rows[v, at, :]
                hit = row_iota == (index >> 7)
                parts = []
                for c in range(3):
                    parts.append(jnp.where(hit, term_high[v, c, at, :], 0.0).astype(BF16))
                    parts.append(jnp.where(hit, term_low[v, c, at, :], 0.0).astype(BF16))
                left.append(jnp.concatenate(parts, axis=0))
                right.append(one_hot(lane_iota == (index & (LANES - 1))))
            acc[...] += lax.dot_general(
                jnp.concatenate(left, axis=1),
                jnp.concatenate(right, axis=1),
                NT,
                preferred_element_type=F32,
            )
            return carry

        lax.fori_loop(0, tri_rows_count // step_rows, scatter_step, 0)
    for c in range(3):
        at = c * 2 * rows
        pay[c] = acc[at : at + rows, :] + acc[at + rows : at + 2 * rows, :]

    for i in range(tiles // 8):
        block = slice(8 * i, 8 * i + 8)
        group = inverse[tiles + 8 * i : tiles + 8 * i + 8, :]
        valid = group > 0.5
        marker = ((group - 1.0) * 256.0 + inverse[block, :]).astype(I32)
        marker = jnp.maximum(marker, 0)
        low = marker & (LANES - 1)
        high = marker >> 7
        found = [jnp.zeros((8, LANES), F32) for _ in range(7)]
        for r in range(rows):
            hit = high == r
            for c in range(7):
                found[c] = jnp.where(hit, lane_pick(pay[c, r : r + 1, :], low), found[c])
        for c in range(7):
            packed_ref[c, block, :] = jnp.where(valid, found[c], -1.0 if c == 6 else 0.0)


def sender(displacement, offsets, cell_local, destination, triangles, stiffness, tiles):
    count = displacement.shape[1]
    tris = triangles.shape[1]
    rows = count // LANES
    return pl.pallas_call(
        sender_kernel,
        out_shape=(
            jax.ShapeDtypeStruct((7, tiles, CAP), F32),
            jax.ShapeDtypeStruct((rows, LANES), I32),
        ),
        in_specs=[pl.BlockSpec(memory_space=pltpu.HBM)] * 6,
        out_specs=(pl.BlockSpec(memory_space=pltpu.VMEM),) * 2,
        scratch_shapes=[
            pltpu.VMEM(displacement.shape, F32),
            pltpu.VMEM(offsets.shape, F32),
            pltpu.VMEM(cell_local.shape, I32),
            pltpu.VMEM(destination.shape, I32),
            pltpu.VMEM(triangles.shape, I32),
            pltpu.VMEM(stiffness.shape, F32),
            pltpu.VMEM((3, rows, LANES), F32),
            pltpu.VMEM((7, rows, LANES), F32),
            pltpu.VMEM((3, tris // LANES, LANES), I32),
            pltpu.VMEM((3, 3, tris // LANES, LANES), F32),
            pltpu.VMEM((3, 3, tris // LANES, LANES), F32),
            pltpu.VMEM((6 * rows, LANES), F32),
            pltpu.VMEM((2 * rows, LANES), F32),
            pltpu.VMEM((rows, LANES), I32),
            pltpu.VMEM((rows, LANES), I32),
            pltpu.VMEM((rows, LANES), I32),
            pltpu.VMEM((tiles, count), BF16),
            pltpu.SemaphoreType.DMA((6,)),
        ],
        compiler_params=pltpu.CompilerParams(vmem_limit_bytes=50 * MIB),
        name="sender",
    )(displacement, offsets, cell_local, destination, triangles, stiffness)


def chunk_rows(arrived, i, channels):
    out = {}
    for c in channels:
        tile = arrived[c, pl.ds(pl.multiple_of(i * RANKS, RANKS), RANKS), :]
        out[c] = jnp.concatenate([tile[r : r + 1, :] for r in range(RANKS)], axis=1)
    return out


def plane_weights(rows):
    cell = rows[6].astype(I32)
    y = (cell >> 8) & 31
    x = cell >> 13
    eight = iota((8, WIDE), 0)
    weight_x = jnp.where(eight == x, 1.0 - rows[3], jnp.where(eight == x + 1, rows[3], 0.0))

    def weight_y(at):
        return jnp.where(y == at, 1.0 - rows[4], jnp.where(y + 1 == at, rows[4], 0.0))

    return weight_x, weight_y


def signed(sign, value):
    return value if sign > 0 else -value


def plus(total, sign, value):
    if total is None:
        return signed(sign, value)
    return total + value if sign > 0 else total - value


def fluid_kernel(
    arrived_ref,
    pops_hbm,
    vel_ref,
    moved_hbm,
    x_plus,
    x_minus,
    y_plus,
    y_minus,
    arrived,
    pops,
    moved,
    field,
    depth_high,
    depth_low,
    vel_high,
    vel_low,
    vel_rows,
    span_rows,
    spans,
    pops_sem,
    span_sem,
    moved_sem,
):
    fetch = pltpu.make_async_copy(pops_hbm, pops, pops_sem)
    fetch.start()
    chunks = CAP // RANKS
    cells_x, cells_y, cells_z = moved.shape[1:]
    for c in range(7):
        arrived[c] = arrived_ref[c].T

    cell = arrived_ref[6].astype(I32)
    y_all = (cell >> 8) & 31
    lowest = jnp.min(jnp.where(cell < 0, 99, y_all), axis=0, keepdims=True)
    highest = jnp.max(jnp.where(cell < 0, -99, y_all), axis=0, keepdims=True)
    extent = jnp.concatenate([lowest] * 8, axis=0)
    extent = jnp.where(iota((8, LANES), 0) == 1, -highest, extent)
    for step in (1, 2, 4):
        extent = jnp.minimum(extent, pltpu.roll(extent, LANES - step, 1))
    span_rows[...] = extent
    share = pltpu.make_async_copy(span_rows, spans, span_sem)
    share.start()
    field[...] = jnp.zeros_like(field)
    depth_iota = iota((cells_z, WIDE), 0)
    span = WINDOW * 24
    share.wait()

    def windows(i):
        start = spans[0, i * RANKS]
        end = 2 - spans[1, i * RANKS]
        return start, jnp.maximum(end - start + WINDOW - 1, 0) // WINDOW

    def spread_step(i, carry):
        rows = chunk_rows(arrived, i, range(7))
        depth = rows[6].astype(I32) & 255
        first = depth_iota == depth
        second = depth_iota == depth + 1
        lower = 1.0 - rows[5]
        lower_high = lower.astype(BF16).astype(F32)
        upper_high = rows[5].astype(BF16).astype(F32)
        depth_high[i] = jnp.where(first, lower_high, jnp.where(second, upper_high, 0.0)).astype(
            BF16
        )
        depth_low[i] = jnp.where(
            first, lower - lower_high, jnp.where(second, rows[5] - upper_high, 0.0)
        ).astype(BF16)
        weight_x, weight_y = plane_weights(rows)
        pushed = [weight_x * rows[c] for c in range(3)]
        start, number = windows(i)

        def window_step(w, carry):
            y_first = start + w * WINDOW
            parts = []
            for y in range(WINDOW):
                at_y = weight_y(y_first + y)
                for c in range(3):
                    parts.append(pushed[c] * at_y)
            spread_high, spread_low = split(jnp.concatenate(parts, axis=0))
            high = depth_high[i]
            add = lax.dot_general(
                jnp.concatenate([spread_high, spread_low, spread_high], axis=1),
                jnp.concatenate([high, high, depth_low[i]], axis=1),
                NT,
                preferred_element_type=F32,
            )
            at = pl.ds(pl.multiple_of(y_first * 24, 8), span)
            field[0, at, :] += add[:, 0:LANES]
            field[1, at, :] += add[:, LANES:]
            return carry

        return lax.fori_loop(0, number, window_step, carry)

    lax.fori_loop(0, chunks, spread_step, 0)

    fetch.wait()
    push = 1.0 - 0.5 / RELAX
    rest = 1.0 - 1.0 / RELAX

    def plane_step(x, carry):
        rho = pops[0, x]
        for q in range(1, 19):
            rho = rho + pops[q, x]
        inverse = 1.0 / rho
        pull = []
        velocity = []
        for c in range(3):
            moment = None
            for q in range(19):
                if LATTICE[q, c] != 0:
                    moment = plus(moment, LATTICE[q, c], pops[q, x])
            at = pl.ds(c * 8 + x, cells_y, stride=24)
            force = jnp.concatenate([field[0, at, :], field[1, at, :]], axis=1)
            flow = (moment + 0.5 * force) * inverse
            field[0, at, :] = flow[:, 0:LANES]
            field[1, at, :] = flow[:, LANES:]
            pull.append(force)
            velocity.append(flow)
        usq = velocity[0] * velocity[0] + velocity[1] * velocity[1] + velocity[2] * velocity[2]
        udotf = velocity[0] * pull[0] + velocity[1] * pull[1] + velocity[2] * pull[2]
        base = rho * (1.0 - 1.5 * usq) * (1.0 / RELAX) - (3.0 * push) * udotf

        def emit(q, value):
            cx, cy, cz = (int(v) for v in LATTICE[q])
            if cy != 0:
                value = pltpu.roll(value, cy % cells_y, 0)
            if cz != 0:
                value = pltpu.roll(value, cz % cells_z, 1)
            to = x + cx
            if cx > 0:
                to = jnp.where(to == cells_x, 0, to)
            if cx < 0:
                to = jnp.where(to < 0, cells_x - 1, to)
            moved[q, to] = value
            pltpu.make_async_copy(moved.at[q, to], moved_hbm.at[q, to], moved_sem).start()

        emit(0, rest * pops[0, x] + LATTICE_WEIGHTS[0] * base)
        for q in range(1, 19, 2):
            along = None
            pulled = None
            for c in range(3):
                if LATTICE[q, c] != 0:
                    along = plus(along, LATTICE[q, c], velocity[c])
                    pulled = plus(pulled, LATTICE[q, c], pull[c])
            odd = (3.0 / RELAX) * rho * along + (3.0 * push) * pulled
            even = base + along * ((4.5 / RELAX) * rho * along + (9.0 * push) * pulled)
            weight = LATTICE_WEIGHTS[q]
            emit(q, rest * pops[q, x] + weight * (even + odd))
            emit(q + 1, rest * pops[q + 1, x] + weight * (even - odd))
        return carry

    lax.fori_loop(0, cells_x, plane_step, 0)
    last_x = cells_x - 1
    last_y = cells_y - 1
    for n in range(5):
        x_plus[n] = moved[X_PLUS[n], 0]
        x_minus[n] = moved[X_MINUS[n], last_x]
        for x in range(cells_x):
            y_plus[n, x : x + 1, :] = moved[Y_PLUS[n], x, 0:1, :]
            y_minus[n, x : x + 1, :] = moved[Y_MINUS[n], x, last_y:, :]
    lines = vel_high.shape[1]
    for odd in range(2):
        for half in range(2):
            lane = slice(half * LANES, half * LANES + LANES)
            high, low = split(field[half, odd * 24 : odd * 24 + lines, :])
            vel_high[odd, :, lane] = high
            vel_low[odd, :, lane] = low

    def gather_step(i, carry):
        rows = chunk_rows(arrived, i, (3, 4, 6))
        weight_x, weight_y = plane_weights(rows)
        start, number = windows(i)

        def window_step(w, sums):
            y_first = start + w * WINDOW
            odd = y_first & 1
            at = pl.ds(pl.multiple_of((y_first - odd) * 24, 16), span)
            upper = vel_high[odd, at, :]
            high = depth_high[i]
            total = jnp.dot(
                jnp.concatenate([upper, vel_low[odd, at, :], upper], axis=1),
                jnp.concatenate([high, high, depth_low[i]], axis=0),
                preferred_element_type=F32,
            )
            sums = list(sums)
            for y in range(WINDOW):
                plane = weight_x * weight_y(y_first + y)
                for c in range(3):
                    line = y * 24 + c * 8
                    sums[c] = sums[c] + plane * total[line : line + 8]
            return tuple(sums)

        zero = jnp.zeros((8, WIDE), F32)
        sums = lax.fori_loop(0, number, window_step, (zero, zero, zero))
        for c in range(3):
            value = jnp.sum(sums[c], axis=0, keepdims=True)
            vel_rows[c, pl.ds(pl.multiple_of(i * RANKS, RANKS), RANKS), :] = jnp.concatenate(
                [value[:, r * LANES : (r + 1) * LANES] for r in range(RANKS)], axis=0
            )
        return carry

    lax.fori_loop(0, chunks, gather_step, 0)
    for c in range(3):
        vel_ref[c] = vel_rows[c].T
    pltpu.make_async_copy(moved, moved_hbm, moved_sem).wait()


def fluid(arrived, populations):
    shape = populations.shape
    _, cells_x, cells_y, cells_z = shape
    sources = arrived.shape[1]
    lines = (cells_y + WINDOW) * 24
    face_x = jax.ShapeDtypeStruct((5, cells_y, cells_z), F32)
    face_y = jax.ShapeDtypeStruct((5, cells_x, cells_z), F32)
    vmem = pl.BlockSpec(memory_space=pltpu.VMEM)
    anywhere = pl.BlockSpec(memory_space=pltpu.HBM)
    return pl.pallas_call(
        fluid_kernel,
        out_shape=(
            jax.ShapeDtypeStruct((3, sources, CAP), F32),
            jax.ShapeDtypeStruct(shape, F32),
            face_x,
            face_x,
            face_y,
            face_y,
        ),
        in_specs=[vmem, anywhere],
        out_specs=(vmem, anywhere, vmem, vmem, vmem, vmem),
        scratch_shapes=[
            pltpu.VMEM((7, CAP, sources), F32),
            pltpu.VMEM(shape, F32),
            pltpu.VMEM(shape, F32),
            pltpu.VMEM((2, lines + 24, LANES), F32),
            pltpu.VMEM((CAP // RANKS, cells_z, WIDE), BF16),
            pltpu.VMEM((CAP // RANKS, cells_z, WIDE), BF16),
            pltpu.VMEM((2, lines, cells_z), BF16),
            pltpu.VMEM((2, lines, cells_z), BF16),
            pltpu.VMEM((3, CAP, sources), F32),
            pltpu.VMEM((8, LANES), I32),
            pltpu.SMEM((8, LANES), I32),
            pltpu.SemaphoreType.DMA,
            pltpu.SemaphoreType.DMA,
            pltpu.SemaphoreType.DMA,
        ],
        compiler_params=pltpu.CompilerParams(vmem_limit_bytes=56 * MIB),
        name="fluid",
    )(arrived, populations)


def patch_x_kernel(
    moved, x_plus, x_minus, y_plus, y_minus, out, y_plus_out, y_minus_out, write_sem
):
    cells_x, cells_y = out.shape[1:3]
    writes = []
    for faces, qs, x in ((x_plus, X_PLUS, 0), (x_minus, X_MINUS, cells_x - 1)):
        for n, q in enumerate(qs):
            copy = pltpu.make_async_copy(faces.at[n], out.at[q, x], write_sem.at[len(writes)])
            copy.start()
            writes.append(copy)
    y_plus_out[...] = y_plus[...]
    y_minus_out[...] = y_minus[...]
    for faces, qs, x in ((x_plus, X_PLUS, 0), (x_minus, X_MINUS, cells_x - 1)):
        for n, q in enumerate(qs):
            if LATTICE[q, 1] > 0:
                y_plus_out[Y_PLUS.index(q), x : x + 1, :] = faces[n, 0:1, :]
            if LATTICE[q, 1] < 0:
                y_minus_out[Y_MINUS.index(q), x : x + 1, :] = faces[n, cells_y - 1 :, :]
    for copy in writes:
        copy.wait()


def patch_x(moved, x_plus, x_minus, y_plus, y_minus):
    vmem = pl.BlockSpec(memory_space=pltpu.VMEM)
    anywhere = pl.BlockSpec(memory_space=pltpu.HBM)
    face = jax.ShapeDtypeStruct(y_plus.shape, F32)
    return pl.pallas_call(
        patch_x_kernel,
        out_shape=(jax.ShapeDtypeStruct(moved.shape, F32), face, face),
        in_specs=[anywhere, vmem, vmem, vmem, vmem],
        out_specs=(anywhere, vmem, vmem),
        scratch_shapes=[pltpu.SemaphoreType.DMA((10,))],
        input_output_aliases={0: 0},
        compiler_params=pltpu.CompilerParams(vmem_limit_bytes=32 * MIB),
        cost_estimate=pl.CostEstimate(
            flops=0, bytes_accessed=16 * x_plus.size, transcendentals=0
        ),
        name="patch_x",
    )(moved, x_plus, x_minus, y_plus, y_minus)


def patch_y_kernel(moved, y_plus, y_minus, out, blocks, read_sem, write_sem):
    cells_x, cells_y = out.shape[1:3]
    reads = []
    for n, q in enumerate(Y_PLUS + Y_MINUS):
        at = 0 if n < 5 else cells_y - 8
        reads.append(
            pltpu.make_async_copy(out.at[q, :, pl.ds(at, 8), :], blocks.at[n], read_sem.at[n])
        )
        reads[-1].start()
    writes = []
    for n, q in enumerate(Y_PLUS + Y_MINUS):
        reads[n].wait()
        faces, row, at = (y_plus, 0, 0) if n < 5 else (y_minus, 7, cells_y - 8)
        for x in range(cells_x):
            blocks[n, x, row : row + 1, :] = faces[n % 5, x : x + 1, :]
        copy = pltpu.make_async_copy(blocks.at[n], out.at[q, :, pl.ds(at, 8), :], write_sem.at[n])
        copy.start()
        writes.append(copy)
    for copy in writes:
        copy.wait()


def patch_y(moved, y_plus, y_minus):
    _, cells_x, cells_y, cells_z = moved.shape
    vmem = pl.BlockSpec(memory_space=pltpu.VMEM)
    anywhere = pl.BlockSpec(memory_space=pltpu.HBM)
    return pl.pallas_call(
        patch_y_kernel,
        out_shape=jax.ShapeDtypeStruct(moved.shape, F32),
        in_specs=[anywhere, vmem, vmem],
        out_specs=anywhere,
        scratch_shapes=[
            pltpu.VMEM((10, cells_x, 8, cells_z), F32),
            pltpu.SemaphoreType.DMA((10,)),
            pltpu.SemaphoreType.DMA((10,)),
        ],
        input_output_aliases={0: 0},
        compiler_params=pltpu.CompilerParams(vmem_limit_bytes=32 * MIB),
        cost_estimate=pl.CostEstimate(
            flops=0, bytes_accessed=80 * cells_x * 8 * cells_z, transcendentals=0
        ),
        name="patch_y",
    )(moved, y_plus, y_minus)


def unpack_kernel(returned, dest_ref, slot_ref, out_ref):
    tiles = returned.shape[1]
    rows = dest_ref.shape[0]
    parts = []
    for c in range(3):
        high, low = split(returned[c])
        parts.append(jnp.concatenate([high, low], axis=1))
    values = jnp.concatenate(parts, axis=0)
    group = 8
    wide = group * LANES
    for b in range(rows // group):
        slot = jnp.concatenate(
            [slot_ref[b * group + r : b * group + r + 1, :] for r in range(group)], axis=1
        )
        dest = jnp.concatenate(
            [dest_ref[b * group + r : b * group + r + 1, :] for r in range(group)], axis=1
        )
        hot = one_hot(slot == iota((CAP, wide), 0))
        picked = jnp.dot(
            values, jnp.concatenate([hot, hot], axis=0), preferred_element_type=F32
        )
        hit = dest == iota((tiles, wide), 0)
        for c in range(3):
            out_ref[c : c + 1, b * wide : (b + 1) * wide] = jnp.sum(
                jnp.where(hit, picked[c * tiles : (c + 1) * tiles, :], 0.0), axis=0, keepdims=True
            )


def unpack(returned, dest, slot):
    count = dest.size
    return pl.pallas_call(
        unpack_kernel,
        out_shape=jax.ShapeDtypeStruct((3, count), F32),
        in_specs=[pl.BlockSpec(memory_space=pltpu.VMEM)] * 3,
        out_specs=pl.BlockSpec(memory_space=pltpu.VMEM),
        compiler_params=pltpu.CompilerParams(vmem_limit_bytes=40 * MIB),
        name="unpack",
    )(returned, dest, slot)


def both_ways(axis, low, high):
    size = lax.axis_size(axis)
    forward = [(i, (i + 1) % size) for i in range(size)]
    backward = [(target, source) for source, target in forward]
    return lax.ppermute(low, axis, forward), lax.ppermute(high, axis, backward)


def shards(populations, displacement, offsets, cell_local, destination, triangles, stiffness):
    tiles = lax.axis_size("gx") * lax.axis_size("gy")
    dest_rows = destination.reshape(-1, LANES)
    packed, slot = sender(
        displacement,
        offsets,
        cell_local,
        dest_rows,
        triangles.T,
        stiffness.reshape(-1, LANES),
        tiles,
    )
    arrived = lax.all_to_all(packed, ("gx", "gy"), split_axis=1, concat_axis=1, tiled=True)
    slot_velocity, moved, x_plus, x_minus, y_plus, y_minus = fluid(arrived, populations)
    returned = lax.all_to_all(slot_velocity, ("gx", "gy"), split_axis=1, concat_axis=1, tiled=True)
    x_plus, x_minus = both_ways("gx", x_plus, x_minus)
    moved, y_plus, y_minus = patch_x(moved, x_plus, x_minus, y_plus, y_minus)
    y_plus, y_minus = both_ways("gy", y_plus, y_minus)
    populations_next = patch_y(moved, y_plus, y_minus)
    marker_velocity = unpack(returned, dest_rows, slot)
    return (populations_next, marker_velocity)


def solution(mesh):
    return jax.shard_map(
        shards,
        mesh=mesh,
        in_specs=(
            P(None, "gx", "gy", None),
            P(None, ("gx", "gy")),
            P(None, ("gx", "gy")),
            P(None, ("gx", "gy")),
            P(("gx", "gy"), None),
            P(("gx", "gy"), None),
            P(("gx", "gy")),
        ),
        out_specs=(P(None, "gx", "gy", None), P(None, ("gx", "gy"))),
        check_vma=False,
    )
```

```python
import jax
import jax.numpy as jnp
import numpy as np
from jax import lax
from jax.experimental import pallas as pl
from jax.experimental.pallas import tpu as pltpu
from jax.sharding import PartitionSpec as P

CAP = 128
LANES = 128
WINDOW = 12
RANKS = 8
WIDE = RANKS * LANES
UNROLL = 4

LATTICE = np.array(
    [
        [0, 0, 0],
        [1, 0, 0],
        [-1, 0, 0],
        [0, 1, 0],
        [0, -1, 0],
        [0, 0, 1],
        [0, 0, -1],
        [1, 1, 0],
        [-1, -1, 0],
        [1, -1, 0],
        [-1, 1, 0],
        [1, 0, 1],
        [-1, 0, -1],
        [1, 0, -1],
        [-1, 0, 1],
        [0, 1, 1],
        [0, -1, -1],
        [0, 1, -1],
        [0, -1, 1],
    ]
)
LATTICE_WEIGHTS = [1.0 / 3.0] + [1.0 / 18.0] * 6 + [1.0 / 36.0] * 12
RELAX = 0.8
X_PLUS = [q for q in range(19) if LATTICE[q, 0] == 1]
X_MINUS = [q for q in range(19) if LATTICE[q, 0] == -1]
Y_PLUS = [q for q in range(19) if LATTICE[q, 1] == 1]
Y_MINUS = [q for q in range(19) if LATTICE[q, 1] == -1]
DIAGONAL = [q for q in range(19) if LATTICE[q, 0] != 0 and LATTICE[q, 1] != 0]
NT = (((1,), (1,)), ((), ()))
F32 = jnp.float32
BF16 = jnp.bfloat16
I32 = jnp.int32
MIB = 1 << 20


def iota(shape, dim):
    return lax.broadcasted_iota(I32, shape, dim)


def split(value):
    high = value.astype(BF16)
    low = (value - high.astype(F32)).astype(BF16)
    return high, low


def one_hot(hit):
    return jnp.where(hit, 1.0, 0.0).astype(BF16)


def lane_pick(row, lanes):
    return jnp.take_along_axis(jnp.broadcast_to(row, lanes.shape), lanes, axis=1)


def sender_kernel(
    disp_hbm,
    offs_hbm,
    cell_hbm,
    dest_hbm,
    tri_hbm,
    stiff_hbm,
    packed_ref,
    slot_ref,
    disp_ref,
    offs_ref,
    cell_ref,
    dest_ref,
    tri_ref,
    stiff_ref,
    disp_rows,
    pay,
    tri_rows,
    term_high,
    term_low,
    acc,
    order,
    place,
    sorted_dest,
    sorted_slot,
    mask,
    sems,
):
    fetches = []
    for n, (source, target) in enumerate(
        (
            (cell_hbm, cell_ref),
            (dest_hbm, dest_ref),
            (tri_hbm, tri_ref),
            (disp_hbm, disp_ref),
            (stiff_hbm, stiff_ref),
            (offs_hbm, offs_ref),
        )
    ):
        fetches.append(pltpu.make_async_copy(source, target, sems.at[n]))
        fetches[-1].start()
    count = disp_ref.shape[1]
    rows = count // LANES
    tri_rows_count = tri_ref.shape[1] // LANES
    tiles = packed_ref.shape[0] // 8
    width = 256
    blocks = count // width
    bins = 32
    for fetch in fetches:
        fetch.wait()
    for r in range(rows):
        lane = pl.ds(r * LANES, LANES)
        flat = (cell_ref[0:1, lane] * 32 + cell_ref[1:2, lane]) * 256 + cell_ref[2:3, lane]
        pay[6, r : r + 1, :] = flat.astype(F32)
        for c in range(3):
            disp_rows[c, r : r + 1, :] = disp_ref[c : c + 1, lane]
            pay[3 + c, r : r + 1, :] = offs_ref[c : c + 1, lane]
    for r in range(tri_rows_count):
        for v in range(3):
            tri_rows[v, r : r + 1, :] = tri_ref[v : v + 1, pl.ds(r * LANES, LANES)]

    earlier = one_hot(iota((width, 2 * width), 0) < iota((width, 2 * width), 1))
    bin_iota = iota((bins, width), 0)
    y_hits = [cell_ref[1:2, b * width : (b + 1) * width] == bin_iota for b in range(blocks)]
    y_counts = jnp.dot(
        jnp.concatenate([one_hot(hit) for hit in y_hits], axis=0),
        earlier,
        preferred_element_type=F32,
    )
    totals = y_counts[0:bins, width:]
    for b in range(1, blocks):
        totals = totals + y_counts[b * bins : (b + 1) * bins, width:]
    below = jnp.where(iota((bins, bins), 1) < iota((bins, bins), 0), 1.0, 0.0)
    first = jnp.dot(below, totals, preferred_element_type=F32, precision=lax.Precision.HIGHEST)
    within = iota((1, width), 1).astype(F32)
    running = first
    left = []
    right = []
    for b in range(blocks):
        own = y_counts[b * bins : (b + 1) * bins, 0:width] + running
        running = running + y_counts[b * bins : (b + 1) * bins, width:]
        at = jnp.sum(jnp.where(y_hits[b], own, 0.0), axis=0, keepdims=True).astype(I32)
        place[2 * b : 2 * b + 1, :] = at[:, 0:LANES]
        place[2 * b + 1 : 2 * b + 2, :] = at[:, LANES:]
        hit = (at >> 7) == iota((rows, width), 0)
        left.append(
            jnp.concatenate(
                [
                    jnp.where(hit, within, 0.0).astype(BF16),
                    jnp.where(hit, float(b), 0.0).astype(BF16),
                ],
                axis=0,
            )
        )
        right.append(one_hot((at & (LANES - 1)) == iota((LANES, width), 0)))
    order[...] = lax.dot_general(
        jnp.concatenate(left, axis=1),
        jnp.concatenate(right, axis=1),
        NT,
        preferred_element_type=F32,
    )
    for i in range(rows // 8):
        block = slice(8 * i, 8 * i + 8)
        marker = (order[rows + 8 * i : rows + 8 * i + 8, :] * 256.0 + order[block, :]).astype(I32)
        low = marker & (LANES - 1)
        high = marker >> 7
        found = jnp.zeros((8, LANES), I32)
        for r in range(rows):
            found = jnp.where(high == r, lane_pick(dest_ref[r : r + 1, :], low), found)
        sorted_dest[block, :] = found

    def row_of(ref, b, at=0):
        return jnp.concatenate(
            [ref[at + 2 * b : at + 2 * b + 1, :], ref[at + 2 * b + 1 : at + 2 * b + 2, :]], axis=1
        )

    tile_iota = iota((tiles, width), 0)
    hots = []
    cums = []
    for b in range(blocks):
        mask[:, b * width : (b + 1) * width] = one_hot(row_of(sorted_dest, b) == tile_iota)
        at = within + float(b * width)
        hots.append((at >= first) & (at < first + totals))
        cums.append(one_hot(at < first))
    before = jnp.dot(
        jnp.concatenate([mask[:, b * width : (b + 1) * width] for b in range(blocks)], axis=0),
        earlier,
        preferred_element_type=F32,
    )
    smaller = lax.dot_general(
        jnp.concatenate(cums, axis=1), mask[...], NT, preferred_element_type=F32
    )
    room = float(CAP) - smaller[bins - 1 : bins, :]
    ahead = jnp.zeros((1, tiles), F32)
    shift = []
    for y in range(bins):
        ahead = jnp.maximum(ahead, float((y * CAP) // (bins - 1)) - smaller[y : y + 1, :])
        shift.append(jnp.minimum(ahead, room))
    shift = jnp.concatenate(shift, axis=0).astype(BF16)
    shifts = jnp.dot(shift, mask[...], preferred_element_type=F32)
    running = jnp.zeros((tiles, width), F32)
    left = []
    right = []
    for b in range(blocks):
        lane = slice(b * width, (b + 1) * width)
        hit = row_of(sorted_dest, b) == tile_iota
        own = before[b * tiles : (b + 1) * tiles, 0:width] + running
        running = running + before[b * tiles : (b + 1) * tiles, width:]
        slot = jnp.sum(jnp.where(hit, own, 0.0), axis=0, keepdims=True) + jnp.sum(
            jnp.where(hots[b], shifts[:, lane], 0.0), axis=0, keepdims=True
        )
        slot = slot.astype(I32)
        sorted_slot[2 * b : 2 * b + 1, :] = slot[:, 0:LANES]
        sorted_slot[2 * b + 1 : 2 * b + 2, :] = slot[:, LANES:]
        left.append(
            jnp.concatenate(
                [
                    jnp.where(hit, row_of(order, b), 0.0).astype(BF16),
                    jnp.where(hit, row_of(order, b, rows) + 1.0, 0.0).astype(BF16),
                ],
                axis=0,
            )
        )
        right.append(one_hot(slot == iota((CAP, width), 0)))
    inverse = lax.dot_general(
        jnp.concatenate(left, axis=1),
        jnp.concatenate(right, axis=1),
        NT,
        preferred_element_type=F32,
    )
    for i in range(rows // 8):
        block = slice(8 * i, 8 * i + 8)
        at = place[block, :]
        low = at & (LANES - 1)
        high = at >> 7
        found = jnp.zeros((8, LANES), I32)
        for r in range(rows):
            found = jnp.where(high == r, lane_pick(sorted_slot[r : r + 1, :], low), found)
        slot_ref[block, :] = found

    def gather_step(i, carry):
        block = pl.ds(i * 8, 8)
        corner = []
        for v in range(3):
            index = tri_rows[v, block, :]
            low = index & (LANES - 1)
            high = index >> 7
            found = [jnp.zeros((8, LANES), F32) for _ in range(3)]
            for r in range(rows):
                hit = high == r
                for c in range(3):
                    found[c] = jnp.where(hit, lane_pick(disp_rows[c, r : r + 1, :], low), found[c])
            corner.append(found)
        stiff = stiff_ref[block, :]
        for c in range(3):
            total = corner[0][c] + corner[1][c] + corner[2][c]
            for v in range(3):
                term = stiff * (total - 3.0 * corner[v][c])
                rounded = term.astype(BF16).astype(F32)
                term_high[v, c, block, :] = rounded
                term_low[v, c, block, :] = term - rounded
        return carry

    for i in range(tri_rows_count // 8):
        gather_step(i, 0)

    acc[...] = jnp.zeros_like(acc)
    row_iota = iota((rows, LANES), 0)
    lane_iota = iota((LANES, LANES), 0)
    step_rows = 32
    for v in range(3):

        def scatter_step(i, carry, v=v):
            left = []
            right = []
            for k in range(step_rows):
                at = pl.ds(i * step_rows + k, 1)
                index = tri_rows[v, at, :]
                hit = row_iota == (index >> 7)
                parts = []
                for c in range(3):
                    parts.append(jnp.where(hit, term_high[v, c, at, :], 0.0).astype(BF16))
                    parts.append(jnp.where(hit, term_low[v, c, at, :], 0.0).astype(BF16))
                left.append(jnp.concatenate(parts, axis=0))
                right.append(one_hot(lane_iota == (index & (LANES - 1))))
            acc[...] += lax.dot_general(
                jnp.concatenate(left, axis=1),
                jnp.concatenate(right, axis=1),
                NT,
                preferred_element_type=F32,
            )
            return carry

        for i in range(tri_rows_count // step_rows):
            scatter_step(i, 0)
    for c in range(3):
        at = c * 2 * rows
        pay[c] = acc[at : at + rows, :] + acc[at + rows : at + 2 * rows, :]

    for i in range(tiles // 8):
        block = slice(8 * i, 8 * i + 8)
        group = inverse[tiles + 8 * i : tiles + 8 * i + 8, :]
        valid = group > 0.5
        marker = ((group - 1.0) * 256.0 + inverse[block, :]).astype(I32)
        marker = jnp.maximum(marker, 0)
        low = marker & (LANES - 1)
        high = marker >> 7
        found = [jnp.zeros((8, LANES), F32) for _ in range(7)]
        for r in range(rows):
            hit = high == r
            for c in range(7):
                found[c] = jnp.where(hit, lane_pick(pay[c, r : r + 1, :], low), found[c])
        for c in range(7):
            value = jnp.where(valid, found[c], -1.0 if c == 6 else 0.0)
            packed_ref[pl.ds(64 * i + c, 8, stride=8), :] = value
        packed_ref[pl.ds(64 * i + 7, 8, stride=8), :] = jnp.zeros((8, LANES), F32)


def sender(displacement, offsets, cell_local, destination, triangles, stiffness, tiles):
    count = displacement.shape[1]
    tris = triangles.shape[1]
    rows = count // LANES
    return pl.pallas_call(
        sender_kernel,
        out_shape=(
            jax.ShapeDtypeStruct((8 * tiles, CAP), F32),
            jax.ShapeDtypeStruct((rows, LANES), I32),
        ),
        in_specs=[pl.BlockSpec(memory_space=pltpu.HBM)] * 6,
        out_specs=(pl.BlockSpec(memory_space=pltpu.VMEM),) * 2,
        scratch_shapes=[
            pltpu.VMEM(displacement.shape, F32),
            pltpu.VMEM(offsets.shape, F32),
            pltpu.VMEM(cell_local.shape, I32),
            pltpu.VMEM(destination.shape, I32),
            pltpu.VMEM(triangles.shape, I32),
            pltpu.VMEM(stiffness.shape, F32),
            pltpu.VMEM((3, rows, LANES), F32),
            pltpu.VMEM((7, rows, LANES), F32),
            pltpu.VMEM((3, tris // LANES, LANES), I32),
            pltpu.VMEM((3, 3, tris // LANES, LANES), F32),
            pltpu.VMEM((3, 3, tris // LANES, LANES), F32),
            pltpu.VMEM((6 * rows, LANES), F32),
            pltpu.VMEM((2 * rows, LANES), F32),
            pltpu.VMEM((rows, LANES), I32),
            pltpu.VMEM((rows, LANES), I32),
            pltpu.VMEM((rows, LANES), I32),
            pltpu.VMEM((tiles, count), BF16),
            pltpu.SemaphoreType.DMA((6,)),
        ],
        compiler_params=pltpu.CompilerParams(vmem_limit_bytes=60 * MIB),
        cost_estimate=pl.CostEstimate(flops=4 << 30, bytes_accessed=1 << 20, transcendentals=0),
        name="sender",
    )(displacement, offsets, cell_local, destination, triangles, stiffness)


def chunk_rows(arrived, i, channels):
    out = {}
    for c in channels:
        tile = arrived[c, pl.ds(pl.multiple_of(i * RANKS, RANKS), RANKS), :]
        out[c] = jnp.concatenate([tile[r : r + 1, :] for r in range(RANKS)], axis=1)
    return out


def plane_weights(rows):
    cell = rows[6].astype(I32)
    y = (cell >> 8) & 31
    x = cell >> 13
    eight = iota((8, WIDE), 0)
    weight_x = jnp.where(eight == x, 1.0 - rows[3], jnp.where(eight == x + 1, rows[3], 0.0))

    def weight_y(first):
        line = iota((16, WIDE), 0) + first
        return jnp.where(y == line, 1.0 - rows[4], jnp.where(y + 1 == line, rows[4], 0.0))

    return weight_x, weight_y


def signed(sign, value):
    return value if sign > 0 else -value


def plus(total, sign, value):
    if total is None:
        return signed(sign, value)
    return total + value if sign > 0 else total - value


def fluid_kernel(
    arrived_ref,
    pops_hbm,
    vel_ref,
    moved_hbm,
    x_plus,
    x_minus,
    y_plus,
    y_minus,
    arrived,
    pops,
    moved,
    field,
    depth_high,
    depth_low,
    vel_high,
    vel_low,
    vel_rows,
    span_rows,
    spans,
    pops_sem,
    span_sem,
    moved_sem,
):
    fetch = pltpu.make_async_copy(pops_hbm, pops, pops_sem)
    fetch.start()
    chunks = CAP // RANKS
    cells_x, cells_y, cells_z = moved.shape[1:]
    sources = arrived_ref.shape[0] // 8
    for c in range(7):
        arrived[c] = arrived_ref[pl.ds(c, sources, stride=8), :].T

    cell = arrived_ref[pl.ds(6, sources, stride=8), :].astype(I32)
    y_all = (cell >> 8) & 31
    lowest = jnp.min(jnp.where(cell < 0, 99, y_all), axis=0, keepdims=True)
    highest = jnp.max(jnp.where(cell < 0, -99, y_all), axis=0, keepdims=True)
    extent = jnp.broadcast_to(lowest, (8, LANES))
    extent = jnp.where(iota((8, LANES), 0) == 1, -highest, extent)
    for step in (1, 2, 4):
        extent = jnp.minimum(extent, pltpu.roll(extent, LANES - step, 1))
    span_rows[...] = extent
    share = pltpu.make_async_copy(span_rows, spans, span_sem)
    share.start()
    field[...] = jnp.zeros_like(field)
    depth_iota = iota((cells_z, WIDE), 0).astype(F32).astype(BF16)
    none = jnp.zeros((), BF16)
    span = WINDOW * 24
    share.wait()

    def windows(i):
        start = jnp.minimum(spans[0, i * RANKS], 31)
        end = 2 - spans[1, i * RANKS]
        return start, jnp.maximum(end - start + WINDOW - 1, 0) // WINDOW

    def spread_part(rows, depth_parts, pushed, weight_y, y_first):
        parts = []
        lines = weight_y(y_first)
        for y in range(WINDOW):
            at_y = lines[y : y + 1, :]
            for c in range(3):
                parts.append(pushed[c] * at_y)
        spread_high, spread_low = split(jnp.concatenate(parts, axis=0))
        high, low = depth_parts
        add = lax.dot_general(
            jnp.concatenate([spread_high, spread_low, spread_high], axis=1),
            jnp.concatenate([high, high, low], axis=1),
            NT,
            preferred_element_type=F32,
        )
        at = pl.ds(pl.multiple_of(y_first * 24, 8), span)
        field[0, at, :] += add[:, 0:LANES]
        field[1, at, :] += add[:, LANES:]

    def spread_step(g, carry):
        work = []
        for k in range(UNROLL):
            i = g * UNROLL + k
            rows = chunk_rows(arrived, i, range(7))
            depth = rows[6].astype(I32) & 255
            first = depth_iota == depth.astype(F32).astype(BF16)
            second = depth_iota == (depth + 1).astype(F32).astype(BF16)
            lower = 1.0 - rows[5]
            lower_high, lower_low = split(lower)
            upper_high, upper_low = split(rows[5])
            high = jnp.where(first, lower_high, jnp.where(second, upper_high, none))
            low = jnp.where(first, lower_low, jnp.where(second, upper_low, none))
            depth_high[i] = high
            depth_low[i] = low
            weight_x, weight_y = plane_weights(rows)
            pushed = [weight_x * rows[c] for c in range(3)]
            start, number = windows(i)
            spread_part(rows, (high, low), pushed, weight_y, start)
            work.append((i, rows, pushed, weight_y, start, number))
        for i, rows, pushed, weight_y, start, number in work:

            def window_step(w, carry):
                spread_part(
                    rows, (depth_high[i], depth_low[i]), pushed, weight_y, start + w * WINDOW
                )
                return carry

            lax.fori_loop(1, number, window_step, 0)
        return carry

    lax.fori_loop(0, chunks // UNROLL, spread_step, 0)

    fetch.wait()
    push = 1.0 - 0.5 / RELAX
    rest = 1.0 - 1.0 / RELAX

    def plane_step(x, carry):
        rho = pops[0, x]
        for q in range(1, 19):
            rho = rho + pops[q, x]
        inverse = 1.0 / rho
        pull = []
        velocity = []
        for c in range(3):
            moment = None
            for q in range(19):
                if LATTICE[q, c] != 0:
                    moment = plus(moment, LATTICE[q, c], pops[q, x])
            at = pl.ds(c * 8 + x, cells_y, stride=24)
            force = jnp.concatenate([field[0, at, :], field[1, at, :]], axis=1)
            flow = (moment + 0.5 * force) * inverse
            field[0, at, :] = flow[:, 0:LANES]
            field[1, at, :] = flow[:, LANES:]
            pull.append(force)
            velocity.append(flow)
        usq = velocity[0] * velocity[0] + velocity[1] * velocity[1] + velocity[2] * velocity[2]
        udotf = velocity[0] * pull[0] + velocity[1] * pull[1] + velocity[2] * pull[2]
        base = rho * (1.0 - 1.5 * usq) * (1.0 / RELAX) - (3.0 * push) * udotf

        def emit(q, value):
            cx, cy, cz = (int(v) for v in LATTICE[q])
            if cy != 0:
                value = pltpu.roll(value, cy % cells_y, 0)
            if cz != 0:
                value = pltpu.roll(value, cz % cells_z, 1)
            to = x + cx
            if cx > 0:
                to = jnp.where(to == cells_x, 0, to)
            if cx < 0:
                to = jnp.where(to < 0, cells_x - 1, to)
            moved[q, to] = value
            pltpu.make_async_copy(moved.at[q, to], moved_hbm.at[q, to], moved_sem).start()

        emit(0, rest * pops[0, x] + LATTICE_WEIGHTS[0] * base)
        for q in range(1, 19, 2):
            along = None
            pulled = None
            for c in range(3):
                if LATTICE[q, c] != 0:
                    along = plus(along, LATTICE[q, c], velocity[c])
                    pulled = plus(pulled, LATTICE[q, c], pull[c])
            odd = (3.0 / RELAX) * rho * along + (3.0 * push) * pulled
            even = base + along * ((4.5 / RELAX) * rho * along + (9.0 * push) * pulled)
            weight = LATTICE_WEIGHTS[q]
            emit(q, rest * pops[q, x] + weight * (even + odd))
            emit(q + 1, rest * pops[q + 1, x] + weight * (even - odd))
        return carry

    lax.fori_loop(0, cells_x, plane_step, 0)
    last_x = cells_x - 1
    last_y = cells_y - 1
    for n in range(5):
        x_plus[n] = moved[X_PLUS[n], 0]
        x_minus[n] = moved[X_MINUS[n], last_x]
        for x in range(cells_x):
            y_plus[n, x : x + 1, :] = moved[Y_PLUS[n], x, 0:1, :]
            y_minus[n, x : x + 1, :] = moved[Y_MINUS[n], x, last_y:, :]
    lines = vel_high.shape[1]
    for odd in range(2):
        for half in range(2):
            lane = slice(half * LANES, half * LANES + LANES)
            high, low = split(field[half, odd * 24 : odd * 24 + lines, :])
            vel_high[odd, :, lane] = high
            vel_low[odd, :, lane] = low

    def gather_part(i, weight_x, weight_y, y_first):
        odd = y_first & 1
        at = pl.ds(pl.multiple_of((y_first - odd) * 24, 16), span)
        upper = vel_high[odd, at, :]
        high = depth_high[i]
        total = jnp.dot(
            jnp.concatenate([upper, vel_low[odd, at, :], upper], axis=1),
            jnp.concatenate([high, high, depth_low[i]], axis=0),
            preferred_element_type=F32,
        )
        sums = [None] * 3
        lines = weight_y(y_first)
        for y in range(WINDOW):
            plane = weight_x * lines[y : y + 1, :]
            for c in range(3):
                line = y * 24 + c * 8
                part = plane * total[line : line + 8]
                sums[c] = part if sums[c] is None else sums[c] + part
        out = []
        for c in range(3):
            value = jnp.sum(sums[c], axis=0, keepdims=True)
            out.append(
                jnp.concatenate(
                    [value[:, r * LANES : (r + 1) * LANES] for r in range(RANKS)], axis=0
                )
            )
        return out

    def gather_step(g, carry):
        work = []
        for k in range(UNROLL):
            i = g * UNROLL + k
            rows = chunk_rows(arrived, i, (3, 4, 6))
            weight_x, weight_y = plane_weights(rows)
            start, number = windows(i)
            at = pl.ds(pl.multiple_of(i * RANKS, RANKS), RANKS)
            values = gather_part(i, weight_x, weight_y, start)
            for c in range(3):
                vel_rows[c, at, :] = values[c]
            work.append((i, at, weight_x, weight_y, start, number))
        for i, at, weight_x, weight_y, start, number in work:

            def window_step(w, carry):
                values = gather_part(i, weight_x, weight_y, start + w * WINDOW)
                for c in range(3):
                    vel_rows[c, at, :] += values[c]
                return carry

            lax.fori_loop(1, number, window_step, 0)
        return carry

    lax.fori_loop(0, chunks // UNROLL, gather_step, 0)
    for c in range(3):
        vel_ref[pl.ds(c, sources, stride=4), :] = vel_rows[c].T
    vel_ref[pl.ds(3, sources, stride=4), :] = jnp.zeros((sources, CAP), F32)
    pltpu.make_async_copy(moved, moved_hbm, moved_sem).wait()


def fluid(arrived, populations):
    shape = populations.shape
    _, cells_x, cells_y, cells_z = shape
    sources = arrived.shape[0] // 8
    lines = (cells_y + WINDOW) * 24
    face_x = jax.ShapeDtypeStruct((5, cells_y, cells_z), F32)
    face_y = jax.ShapeDtypeStruct((5, cells_x, cells_z), F32)
    vmem = pl.BlockSpec(memory_space=pltpu.VMEM)
    anywhere = pl.BlockSpec(memory_space=pltpu.HBM)
    return pl.pallas_call(
        fluid_kernel,
        out_shape=(
            jax.ShapeDtypeStruct((4 * sources, CAP), F32),
            jax.ShapeDtypeStruct(shape, F32),
            face_x,
            face_x,
            face_y,
            face_y,
        ),
        in_specs=[vmem, anywhere],
        out_specs=(vmem, anywhere, vmem, vmem, vmem, vmem),
        scratch_shapes=[
            pltpu.VMEM((7, CAP, sources), F32),
            pltpu.VMEM(shape, F32),
            pltpu.VMEM(shape, F32),
            pltpu.VMEM((2, lines + 24, LANES), F32),
            pltpu.VMEM((CAP // RANKS, cells_z, WIDE), BF16),
            pltpu.VMEM((CAP // RANKS, cells_z, WIDE), BF16),
            pltpu.VMEM((2, lines, cells_z), BF16),
            pltpu.VMEM((2, lines, cells_z), BF16),
            pltpu.VMEM((3, CAP, sources), F32),
            pltpu.VMEM((8, LANES), I32),
            pltpu.SMEM((8, LANES), I32),
            pltpu.SemaphoreType.DMA,
            pltpu.SemaphoreType.DMA,
            pltpu.SemaphoreType.DMA,
        ],
        compiler_params=pltpu.CompilerParams(vmem_limit_bytes=60 * MIB),
        name="fluid",
    )(arrived, populations)


def patch_x_kernel(
    moved, x_plus, x_minus, y_plus, y_minus, out, y_plus_out, y_minus_out, write_sem
):
    cells_x, cells_y = out.shape[1:3]
    writes = []
    for faces, qs, x in ((x_plus, X_PLUS, 0), (x_minus, X_MINUS, cells_x - 1)):
        for n, q in enumerate(qs):
            copy = pltpu.make_async_copy(faces.at[n], out.at[q, x], write_sem.at[len(writes)])
            copy.start()
            writes.append(copy)
    y_plus_out[...] = y_plus[...]
    y_minus_out[...] = y_minus[...]
    for faces, qs, x in ((x_plus, X_PLUS, 0), (x_minus, X_MINUS, cells_x - 1)):
        for n, q in enumerate(qs):
            if LATTICE[q, 1] > 0:
                y_plus_out[Y_PLUS.index(q), x : x + 1, :] = faces[n, 0:1, :]
            if LATTICE[q, 1] < 0:
                y_minus_out[Y_MINUS.index(q), x : x + 1, :] = faces[n, cells_y - 1 :, :]
    for copy in writes:
        copy.wait()


def patch_x(moved, x_plus, x_minus, y_plus, y_minus):
    vmem = pl.BlockSpec(memory_space=pltpu.VMEM)
    anywhere = pl.BlockSpec(memory_space=pltpu.HBM)
    face = jax.ShapeDtypeStruct(y_plus.shape, F32)
    return pl.pallas_call(
        patch_x_kernel,
        out_shape=(jax.ShapeDtypeStruct(moved.shape, F32), face, face),
        in_specs=[anywhere, vmem, vmem, vmem, vmem],
        out_specs=(anywhere, vmem, vmem),
        scratch_shapes=[pltpu.SemaphoreType.DMA((10,))],
        input_output_aliases={0: 0},
        compiler_params=pltpu.CompilerParams(vmem_limit_bytes=32 * MIB),
        cost_estimate=pl.CostEstimate(
            flops=0, bytes_accessed=16 * x_plus.size, transcendentals=0
        ),
        name="patch_x",
    )(moved, x_plus, x_minus, y_plus, y_minus)


def patch_y_kernel(moved, y_plus, y_minus, out, done, blocks, read_sem, write_sem):
    done[...] = jnp.zeros_like(done)
    cells_x, cells_y = out.shape[1:3]
    reads = []
    for n, q in enumerate(Y_PLUS + Y_MINUS):
        at = 0 if n < 5 else cells_y - 8
        reads.append(
            pltpu.make_async_copy(out.at[q, :, pl.ds(at, 8), :], blocks.at[n], read_sem.at[n])
        )
        reads[-1].start()
    writes = []
    for n, q in enumerate(Y_PLUS + Y_MINUS):
        reads[n].wait()
        faces, row, at = (y_plus, 0, 0) if n < 5 else (y_minus, 7, cells_y - 8)
        for x in range(cells_x):
            blocks[n, x, row : row + 1, :] = faces[n % 5, x : x + 1, :]
        copy = pltpu.make_async_copy(blocks.at[n], out.at[q, :, pl.ds(at, 8), :], write_sem.at[n])
        copy.start()
        writes.append(copy)
    for copy in writes:
        copy.wait()


def patch_y(moved, y_plus, y_minus):
    _, cells_x, cells_y, cells_z = moved.shape
    vmem = pl.BlockSpec(memory_space=pltpu.VMEM)
    anywhere = pl.BlockSpec(memory_space=pltpu.HBM)
    return pl.pallas_call(
        patch_y_kernel,
        out_shape=(
            jax.ShapeDtypeStruct(moved.shape, F32),
            jax.ShapeDtypeStruct((8, LANES), F32),
        ),
        in_specs=[anywhere, vmem, vmem],
        out_specs=(anywhere, vmem),
        scratch_shapes=[
            pltpu.VMEM((10, cells_x, 8, cells_z), F32),
            pltpu.SemaphoreType.DMA((10,)),
            pltpu.SemaphoreType.DMA((10,)),
        ],
        input_output_aliases={0: 0},
        compiler_params=pltpu.CompilerParams(vmem_limit_bytes=32 * MIB),
        cost_estimate=pl.CostEstimate(
            flops=0, bytes_accessed=80 * cells_x * 8 * cells_z, transcendentals=0
        ),
        name="patch_y",
    )(moved, y_plus, y_minus)


def unpack_kernel(returned, dest_ref, slot_ref, later, out_ref):
    tiles = returned.shape[0] // 4
    rows = dest_ref.shape[0]
    parts = []
    for c in range(3):
        high, low = split(returned[pl.ds(c, tiles, stride=4), :])
        parts.append(jnp.concatenate([high, low], axis=1))
    values = jnp.concatenate(parts, axis=0)
    group = 8
    wide = group * LANES
    for b in range(rows // group):
        slot = jnp.concatenate(
            [slot_ref[b * group + r : b * group + r + 1, :] for r in range(group)], axis=1
        )
        dest = jnp.concatenate(
            [dest_ref[b * group + r : b * group + r + 1, :] for r in range(group)], axis=1
        )
        hot = one_hot(slot == iota((CAP, wide), 0))
        picked = jnp.dot(
            values, jnp.concatenate([hot, hot], axis=0), preferred_element_type=F32
        )
        hit = dest == iota((tiles, wide), 0)
        for c in range(3):
            out_ref[c : c + 1, b * wide : (b + 1) * wide] = jnp.sum(
                jnp.where(hit, picked[c * tiles : (c + 1) * tiles, :], 0.0), axis=0, keepdims=True
            )


def unpack(returned, dest, slot, later):
    count = dest.size
    return pl.pallas_call(
        unpack_kernel,
        out_shape=jax.ShapeDtypeStruct((3, count), F32),
        in_specs=[pl.BlockSpec(memory_space=pltpu.VMEM)] * 4,
        out_specs=pl.BlockSpec(memory_space=pltpu.VMEM),
        compiler_params=pltpu.CompilerParams(vmem_limit_bytes=60 * MIB),
        name="unpack",
    )(returned, dest, slot, later)


def to_all(rows, tiles):
    blocks = rows.reshape(tiles, -1, CAP)
    blocks = lax.all_to_all(blocks, ("gx", "gy"), split_axis=0, concat_axis=0, tiled=True)
    return blocks.reshape(-1, CAP)


def both_ways(axis, low, high):
    size = lax.axis_size(axis)
    forward = [(i, (i + 1) % size) for i in range(size)]
    backward = [(target, source) for source, target in forward]
    return lax.ppermute(low, axis, forward), lax.ppermute(high, axis, backward)


def shards(populations, displacement, offsets, cell_local, destination, triangles, stiffness):
    tiles = lax.axis_size("gx") * lax.axis_size("gy")
    dest_rows = destination.reshape(-1, LANES)
    packed, slot = sender(
        displacement,
        offsets,
        cell_local,
        dest_rows,
        triangles.T,
        stiffness.reshape(-1, LANES),
        tiles,
    )
    arrived = to_all(packed, tiles)
    slot_velocity, moved, x_plus, x_minus, y_plus, y_minus = fluid(arrived, populations)
    returned = to_all(slot_velocity, tiles)
    x_plus, x_minus = both_ways("gx", x_plus, x_minus)
    moved, y_plus, y_minus = patch_x(moved, x_plus, x_minus, y_plus, y_minus)
    y_plus, y_minus = both_ways("gy", y_plus, y_minus)
    populations_next, done = patch_y(moved, y_plus, y_minus)
    marker_velocity = unpack(returned, dest_rows, slot, done)
    return (populations_next, marker_velocity)


def solution(mesh):
    return jax.shard_map(
        shards,
        mesh=mesh,
        in_specs=(
            P(None, "gx", "gy", None),
            P(None, ("gx", "gy")),
            P(None, ("gx", "gy")),
            P(None, ("gx", "gy")),
            P(("gx", "gy"), None),
            P(("gx", "gy"), None),
            P(("gx", "gy")),
        ),
        out_specs=(P(None, "gx", "gy", None), P(None, ("gx", "gy"))),
        check_vma=False,
    )
```

```python
import jax
import jax.numpy as jnp
import numpy as np
from jax import lax
from jax.experimental import pallas as pl
from jax.experimental.pallas import tpu as pltpu
from jax.sharding import PartitionSpec as P

CAP = 128
LANES = 128
WINDOW = 12
RANKS = 8
WIDE = RANKS * LANES
UNROLL = 4

LATTICE = np.array(
    [
        [0, 0, 0],
        [1, 0, 0],
        [-1, 0, 0],
        [0, 1, 0],
        [0, -1, 0],
        [0, 0, 1],
        [0, 0, -1],
        [1, 1, 0],
        [-1, -1, 0],
        [1, -1, 0],
        [-1, 1, 0],
        [1, 0, 1],
        [-1, 0, -1],
        [1, 0, -1],
        [-1, 0, 1],
        [0, 1, 1],
        [0, -1, -1],
        [0, 1, -1],
        [0, -1, 1],
    ]
)
LATTICE_WEIGHTS = [1.0 / 3.0] + [1.0 / 18.0] * 6 + [1.0 / 36.0] * 12
RELAX = 0.8
X_PLUS = [q for q in range(19) if LATTICE[q, 0] == 1]
X_MINUS = [q for q in range(19) if LATTICE[q, 0] == -1]
Y_PLUS = [q for q in range(19) if LATTICE[q, 1] == 1]
Y_MINUS = [q for q in range(19) if LATTICE[q, 1] == -1]
DIAGONAL = [q for q in range(19) if LATTICE[q, 0] != 0 and LATTICE[q, 1] != 0]
NT = (((1,), (1,)), ((), ()))
F32 = jnp.float32
BF16 = jnp.bfloat16
I32 = jnp.int32
MIB = 1 << 20


def iota(shape, dim):
    return lax.broadcasted_iota(I32, shape, dim)


def split(value):
    high = value.astype(BF16)
    low = (value - high.astype(F32)).astype(BF16)
    return high, low


def one_hot(hit):
    return jnp.where(hit, 1.0, 0.0).astype(BF16)


def lane_pick(row, lanes):
    return jnp.take_along_axis(jnp.broadcast_to(row, lanes.shape), lanes, axis=1)


def sender_kernel(
    disp_hbm,
    offs_hbm,
    cell_hbm,
    dest_hbm,
    tri_hbm,
    stiff_hbm,
    packed_ref,
    slot_ref,
    disp_ref,
    offs_ref,
    cell_ref,
    dest_ref,
    tri_ref,
    stiff_ref,
    disp_rows,
    pay,
    tri_rows,
    term_high,
    term_low,
    acc,
    order,
    place,
    sorted_dest,
    sorted_slot,
    mask,
    sems,
):
    fetches = []
    for n, (source, target) in enumerate(
        (
            (cell_hbm, cell_ref),
            (dest_hbm, dest_ref),
            (tri_hbm, tri_ref),
            (disp_hbm, disp_ref),
            (stiff_hbm, stiff_ref),
            (offs_hbm, offs_ref),
        )
    ):
        fetches.append(pltpu.make_async_copy(source, target, sems.at[n]))
        fetches[-1].start()
    count = disp_ref.shape[1]
    rows = count // LANES
    tri_rows_count = tri_ref.shape[1] // LANES
    tiles = packed_ref.shape[0] // 8
    width = 256
    blocks = count // width
    bins = 32
    for fetch in fetches:
        fetch.wait()
    for r in range(rows):
        lane = pl.ds(r * LANES, LANES)
        flat = (cell_ref[0:1, lane] * 32 + cell_ref[1:2, lane]) * 256 + cell_ref[2:3, lane]
        pay[6, r : r + 1, :] = flat.astype(F32)
        for c in range(3):
            disp_rows[c, r : r + 1, :] = disp_ref[c : c + 1, lane]
            pay[3 + c, r : r + 1, :] = offs_ref[c : c + 1, lane]
    for r in range(tri_rows_count):
        for v in range(3):
            tri_rows[v, r : r + 1, :] = tri_ref[v : v + 1, pl.ds(r * LANES, LANES)]

    earlier = one_hot(iota((width, 2 * width), 0) < iota((width, 2 * width), 1))
    bin_iota = iota((bins, width), 0)
    y_hits = [cell_ref[1:2, b * width : (b + 1) * width] == bin_iota for b in range(blocks)]
    y_counts = jnp.dot(
        jnp.concatenate([one_hot(hit) for hit in y_hits], axis=0),
        earlier,
        preferred_element_type=F32,
    )
    totals = y_counts[0:bins, width:]
    for b in range(1, blocks):
        totals = totals + y_counts[b * bins : (b + 1) * bins, width:]
    below = jnp.where(iota((bins, bins), 1) < iota((bins, bins), 0), 1.0, 0.0)
    first = jnp.dot(below, totals, preferred_element_type=F32, precision=lax.Precision.HIGHEST)
    within = iota((1, width), 1).astype(F32)
    running = first
    left = []
    right = []
    for b in range(blocks):
        own = y_counts[b * bins : (b + 1) * bins, 0:width] + running
        running = running + y_counts[b * bins : (b + 1) * bins, width:]
        at = jnp.sum(jnp.where(y_hits[b], own, 0.0), axis=0, keepdims=True).astype(I32)
        place[2 * b : 2 * b + 1, :] = at[:, 0:LANES]
        place[2 * b + 1 : 2 * b + 2, :] = at[:, LANES:]
        hit = (at >> 7) == iota((rows, width), 0)
        left.append(
            jnp.concatenate(
                [
                    jnp.where(hit, within, 0.0).astype(BF16),
                    jnp.where(hit, float(b), 0.0).astype(BF16),
                ],
                axis=0,
            )
        )
        right.append(one_hot((at & (LANES - 1)) == iota((LANES, width), 0)))
    order[...] = lax.dot_general(
        jnp.concatenate(left, axis=1),
        jnp.concatenate(right, axis=1),
        NT,
        preferred_element_type=F32,
    )
    for i in range(rows // 8):
        block = slice(8 * i, 8 * i + 8)
        marker = (order[rows + 8 * i : rows + 8 * i + 8, :] * 256.0 + order[block, :]).astype(I32)
        low = marker & (LANES - 1)
        high = marker >> 7
        found = jnp.zeros((8, LANES), I32)
        for r in range(rows):
            found = jnp.where(high == r, lane_pick(dest_ref[r : r + 1, :], low), found)
        sorted_dest[block, :] = found

    def row_of(ref, b, at=0):
        return jnp.concatenate(
            [ref[at + 2 * b : at + 2 * b + 1, :], ref[at + 2 * b + 1 : at + 2 * b + 2, :]], axis=1
        )

    tile_iota = iota((tiles, width), 0)
    hots = []
    cums = []
    for b in range(blocks):
        mask[:, b * width : (b + 1) * width] = one_hot(row_of(sorted_dest, b) == tile_iota)
        at = within + float(b * width)
        hots.append((at >= first) & (at < first + totals))
        cums.append(one_hot(at < first))
    before = jnp.dot(
        jnp.concatenate([mask[:, b * width : (b + 1) * width] for b in range(blocks)], axis=0),
        earlier,
        preferred_element_type=F32,
    )
    smaller = lax.dot_general(
        jnp.concatenate(cums, axis=1), mask[...], NT, preferred_element_type=F32
    )
    room = float(CAP) - smaller[bins - 1 : bins, :]
    ahead = jnp.zeros((1, tiles), F32)
    shift = []
    for y in range(bins):
        ahead = jnp.maximum(ahead, float((y * CAP) // (bins - 1)) - smaller[y : y + 1, :])
        shift.append(jnp.minimum(ahead, room))
    shift = jnp.concatenate(shift, axis=0).astype(BF16)
    shifts = jnp.dot(shift, mask[...], preferred_element_type=F32)
    running = jnp.zeros((tiles, width), F32)
    left = []
    right = []
    for b in range(blocks):
        lane = slice(b * width, (b + 1) * width)
        hit = row_of(sorted_dest, b) == tile_iota
        own = before[b * tiles : (b + 1) * tiles, 0:width] + running
        running = running + before[b * tiles : (b + 1) * tiles, width:]
        slot = jnp.sum(jnp.where(hit, own, 0.0), axis=0, keepdims=True) + jnp.sum(
            jnp.where(hots[b], shifts[:, lane], 0.0), axis=0, keepdims=True
        )
        slot = slot.astype(I32)
        sorted_slot[2 * b : 2 * b + 1, :] = slot[:, 0:LANES]
        sorted_slot[2 * b + 1 : 2 * b + 2, :] = slot[:, LANES:]
        left.append(
            jnp.concatenate(
                [
                    jnp.where(hit, row_of(order, b), 0.0).astype(BF16),
                    jnp.where(hit, row_of(order, b, rows) + 1.0, 0.0).astype(BF16),
                ],
                axis=0,
            )
        )
        right.append(one_hot(slot == iota((CAP, width), 0)))
    inverse = lax.dot_general(
        jnp.concatenate(left, axis=1),
        jnp.concatenate(right, axis=1),
        NT,
        preferred_element_type=F32,
    )
    for i in range(rows // 8):
        block = slice(8 * i, 8 * i + 8)
        at = place[block, :]
        low = at & (LANES - 1)
        high = at >> 7
        found = jnp.zeros((8, LANES), I32)
        for r in range(rows):
            found = jnp.where(high == r, lane_pick(sorted_slot[r : r + 1, :], low), found)
        slot_ref[block, :] = found

    def gather_step(i, carry):
        block = pl.ds(i * 8, 8)
        corner = []
        for v in range(3):
            index = tri_rows[v, block, :]
            low = index & (LANES - 1)
            high = index >> 7
            found = [jnp.zeros((8, LANES), F32) for _ in range(3)]
            for r in range(rows):
                hit = high == r
                for c in range(3):
                    found[c] = jnp.where(hit, lane_pick(disp_rows[c, r : r + 1, :], low), found[c])
            corner.append(found)
        stiff = stiff_ref[block, :]
        for c in range(3):
            total = corner[0][c] + corner[1][c] + corner[2][c]
            for v in range(3):
                term = stiff * (total - 3.0 * corner[v][c])
                rounded = term.astype(BF16).astype(F32)
                term_high[v, c, block, :] = rounded
                term_low[v, c, block, :] = term - rounded
        return carry

    for i in range(tri_rows_count // 8):
        gather_step(i, 0)

    acc[...] = jnp.zeros_like(acc)
    row_iota = iota((rows, LANES), 0)
    lane_iota = iota((LANES, LANES), 0)
    step_rows = 32
    for v in range(3):

        def scatter_step(i, carry, v=v):
            left = []
            right = []
            for k in range(step_rows):
                at = pl.ds(i * step_rows + k, 1)
                index = tri_rows[v, at, :]
                hit = row_iota == (index >> 7)
                parts = []
                for c in range(3):
                    parts.append(jnp.where(hit, term_high[v, c, at, :], 0.0).astype(BF16))
                    parts.append(jnp.where(hit, term_low[v, c, at, :], 0.0).astype(BF16))
                left.append(jnp.concatenate(parts, axis=0))
                right.append(one_hot(lane_iota == (index & (LANES - 1))))
            acc[...] += lax.dot_general(
                jnp.concatenate(left, axis=1),
                jnp.concatenate(right, axis=1),
                NT,
                preferred_element_type=F32,
            )
            return carry

        for i in range(tri_rows_count // step_rows):
            scatter_step(i, 0)
    for c in range(3):
        at = c * 2 * rows
        pay[c] = acc[at : at + rows, :] + acc[at + rows : at + 2 * rows, :]

    for i in range(tiles // 8):
        block = slice(8 * i, 8 * i + 8)
        group = inverse[tiles + 8 * i : tiles + 8 * i + 8, :]
        valid = group > 0.5
        marker = ((group - 1.0) * 256.0 + inverse[block, :]).astype(I32)
        marker = jnp.maximum(marker, 0)
        low = marker & (LANES - 1)
        high = marker >> 7
        found = [jnp.zeros((8, LANES), F32) for _ in range(7)]
        for r in range(rows):
            hit = high == r
            for c in range(7):
                found[c] = jnp.where(hit, lane_pick(pay[c, r : r + 1, :], low), found[c])
        for c in range(7):
            value = jnp.where(valid, found[c], -1.0 if c == 6 else 0.0)
            packed_ref[pl.ds(64 * i + c, 8, stride=8), :] = value
        packed_ref[pl.ds(64 * i + 7, 8, stride=8), :] = jnp.zeros((8, LANES), F32)


def sender(displacement, offsets, cell_local, destination, triangles, stiffness, tiles):
    count = displacement.shape[1]
    tris = triangles.shape[1]
    rows = count // LANES
    return pl.pallas_call(
        sender_kernel,
        out_shape=(
            jax.ShapeDtypeStruct((8 * tiles, CAP), F32),
            jax.ShapeDtypeStruct((rows, LANES), I32),
        ),
        in_specs=[pl.BlockSpec(memory_space=pltpu.HBM)] * 6,
        out_specs=(pl.BlockSpec(memory_space=pltpu.VMEM),) * 2,
        scratch_shapes=[
            pltpu.VMEM(displacement.shape, F32),
            pltpu.VMEM(offsets.shape, F32),
            pltpu.VMEM(cell_local.shape, I32),
            pltpu.VMEM(destination.shape, I32),
            pltpu.VMEM(triangles.shape, I32),
            pltpu.VMEM(stiffness.shape, F32),
            pltpu.VMEM((3, rows, LANES), F32),
            pltpu.VMEM((7, rows, LANES), F32),
            pltpu.VMEM((3, tris // LANES, LANES), I32),
            pltpu.VMEM((3, 3, tris // LANES, LANES), F32),
            pltpu.VMEM((3, 3, tris // LANES, LANES), F32),
            pltpu.VMEM((6 * rows, LANES), F32),
            pltpu.VMEM((2 * rows, LANES), F32),
            pltpu.VMEM((rows, LANES), I32),
            pltpu.VMEM((rows, LANES), I32),
            pltpu.VMEM((rows, LANES), I32),
            pltpu.VMEM((tiles, count), BF16),
            pltpu.SemaphoreType.DMA((6,)),
        ],
        compiler_params=pltpu.CompilerParams(vmem_limit_bytes=60 * MIB),
        cost_estimate=pl.CostEstimate(flops=4 << 30, bytes_accessed=1 << 20, transcendentals=0),
        name="sender",
    )(displacement, offsets, cell_local, destination, triangles, stiffness)


def chunk_rows(arrived, i, channels):
    out = {}
    for c in channels:
        tile = arrived[c, pl.ds(pl.multiple_of(i * RANKS, RANKS), RANKS), :]
        out[c] = jnp.concatenate([tile[r : r + 1, :] for r in range(RANKS)], axis=1)
    return out


def plane_weights(rows):
    cell = rows[6].astype(I32)
    y = (cell >> 8) & 31
    x = cell >> 13
    eight = iota((8, WIDE), 0)
    weight_x = jnp.where(eight == x, 1.0 - rows[3], jnp.where(eight == x + 1, rows[3], 0.0))

    def weight_y(first):
        line = iota((16, WIDE), 0) + first
        return jnp.where(y == line, 1.0 - rows[4], jnp.where(y + 1 == line, rows[4], 0.0))

    return weight_x, weight_y


def depth_weights(rows, depth_iota):
    depth = rows[6].astype(I32) & 255
    first = depth_iota == depth.astype(F32).astype(BF16)
    second = depth_iota == (depth + 1).astype(F32).astype(BF16)
    lower_high, lower_low = split(1.0 - rows[5])
    upper_high, upper_low = split(rows[5])
    none = jnp.zeros((), BF16)
    high = jnp.where(first, lower_high, jnp.where(second, upper_high, none))
    low = jnp.where(first, lower_low, jnp.where(second, upper_low, none))
    return high, low


def windows(spans, i):
    start = jnp.minimum(spans[0, i * RANKS], 31)
    end = 2 - spans[1, i * RANKS]
    return start, jnp.maximum(end - start + WINDOW - 1, 0) // WINDOW


def signed(sign, value):
    return value if sign > 0 else -value


def plus(total, sign, value):
    if total is None:
        return signed(sign, value)
    return total + value if sign > 0 else total - value


def fluid_kernel(
    arrived_ref,
    pops_hbm,
    field,
    span_rows,
    moved_hbm,
    x_plus,
    x_minus,
    y_plus,
    y_minus,
    arrived,
    pops,
    moved,
    depth_high,
    depth_low,
    spans,
    pops_sem,
    span_sem,
    moved_sem,
):
    fetch = pltpu.make_async_copy(pops_hbm, pops, pops_sem)
    fetch.start()
    chunks = CAP // RANKS
    cells_x, cells_y, cells_z = moved.shape[1:]
    sources = arrived_ref.shape[0] // 8
    for c in range(7):
        arrived[c] = arrived_ref[pl.ds(c, sources, stride=8), :].T

    cell = arrived_ref[pl.ds(6, sources, stride=8), :].astype(I32)
    y_all = (cell >> 8) & 31
    lowest = jnp.min(jnp.where(cell < 0, 99, y_all), axis=0, keepdims=True)
    highest = jnp.max(jnp.where(cell < 0, -99, y_all), axis=0, keepdims=True)
    extent = jnp.broadcast_to(lowest, (8, LANES))
    extent = jnp.where(iota((8, LANES), 0) == 1, -highest, extent)
    for step in (1, 2, 4):
        extent = jnp.minimum(extent, pltpu.roll(extent, LANES - step, 1))
    span_rows[...] = extent
    share = pltpu.make_async_copy(span_rows, spans, span_sem)
    share.start()
    field[...] = jnp.zeros_like(field)
    depth_iota = iota((cells_z, WIDE), 0).astype(F32).astype(BF16)
    span = WINDOW * 24
    share.wait()

    def spread_part(rows, depth_parts, pushed, weight_y, y_first):
        parts = []
        lines = weight_y(y_first)
        for y in range(WINDOW):
            at_y = lines[y : y + 1, :]
            for c in range(3):
                parts.append(pushed[c] * at_y)
        spread_high, spread_low = split(jnp.concatenate(parts, axis=0))
        high, low = depth_parts
        add = lax.dot_general(
            jnp.concatenate([spread_high, spread_low, spread_high], axis=1),
            jnp.concatenate([high, high, low], axis=1),
            NT,
            preferred_element_type=F32,
        )
        at = pl.ds(pl.multiple_of(y_first * 24, 8), span)
        field[0, at, :] += add[:, 0:LANES]
        field[1, at, :] += add[:, LANES:]

    def spread_step(g, carry):
        work = []
        for k in range(UNROLL):
            i = g * UNROLL + k
            rows = chunk_rows(arrived, i, range(7))
            high, low = depth_weights(rows, depth_iota)
            depth_high[k] = high
            depth_low[k] = low
            weight_x, weight_y = plane_weights(rows)
            pushed = [weight_x * rows[c] for c in range(3)]
            start, number = windows(spans, i)
            spread_part(rows, (high, low), pushed, weight_y, start)
            work.append((k, rows, pushed, weight_y, start, number))
        for k, rows, pushed, weight_y, start, number in work:

            def window_step(w, carry, k=k, rows=rows, pushed=pushed, weight_y=weight_y, start=start):
                spread_part(
                    rows, (depth_high[k], depth_low[k]), pushed, weight_y, start + w * WINDOW
                )
                return carry

            lax.fori_loop(1, number, window_step, 0)
        return carry

    lax.fori_loop(0, chunks // UNROLL, spread_step, 0)

    fetch.wait()
    push = 1.0 - 0.5 / RELAX
    rest = 1.0 - 1.0 / RELAX

    def plane_step(x, carry):
        rho = pops[0, x]
        for q in range(1, 19):
            rho = rho + pops[q, x]
        inverse = 1.0 / rho
        pull = []
        velocity = []
        for c in range(3):
            moment = None
            for q in range(19):
                if LATTICE[q, c] != 0:
                    moment = plus(moment, LATTICE[q, c], pops[q, x])
            at = pl.ds(c * 8 + x, cells_y, stride=24)
            force = jnp.concatenate([field[0, at, :], field[1, at, :]], axis=1)
            flow = (moment + 0.5 * force) * inverse
            field[0, at, :] = flow[:, 0:LANES]
            field[1, at, :] = flow[:, LANES:]
            pull.append(force)
            velocity.append(flow)
        usq = velocity[0] * velocity[0] + velocity[1] * velocity[1] + velocity[2] * velocity[2]
        udotf = velocity[0] * pull[0] + velocity[1] * pull[1] + velocity[2] * pull[2]
        base = rho * (1.0 - 1.5 * usq) * (1.0 / RELAX) - (3.0 * push) * udotf

        def emit(q, value):
            cx, cy, cz = (int(v) for v in LATTICE[q])
            if cy != 0:
                value = pltpu.roll(value, cy % cells_y, 0)
            if cz != 0:
                value = pltpu.roll(value, cz % cells_z, 1)
            to = x + cx
            if cx > 0:
                to = jnp.where(to == cells_x, 0, to)
            if cx < 0:
                to = jnp.where(to < 0, cells_x - 1, to)
            moved[q, to] = value
            pltpu.make_async_copy(moved.at[q, to], moved_hbm.at[q, to], moved_sem).start()

        emit(0, rest * pops[0, x] + LATTICE_WEIGHTS[0] * base)
        for q in range(1, 19, 2):
            along = None
            pulled = None
            for c in range(3):
                if LATTICE[q, c] != 0:
                    along = plus(along, LATTICE[q, c], velocity[c])
                    pulled = plus(pulled, LATTICE[q, c], pull[c])
            odd = (3.0 / RELAX) * rho * along + (3.0 * push) * pulled
            even = base + along * ((4.5 / RELAX) * rho * along + (9.0 * push) * pulled)
            weight = LATTICE_WEIGHTS[q]
            emit(q, rest * pops[q, x] + weight * (even + odd))
            emit(q + 1, rest * pops[q + 1, x] + weight * (even - odd))
        return carry

    lax.fori_loop(0, cells_x, plane_step, 0)
    last_x = cells_x - 1
    last_y = cells_y - 1
    for n in range(5):
        x_plus[n] = moved[X_PLUS[n], 0]
        x_minus[n] = moved[X_MINUS[n], last_x]
        for x in range(cells_x):
            y_plus[n, x : x + 1, :] = moved[Y_PLUS[n], x, 0:1, :]
            y_minus[n, x : x + 1, :] = moved[Y_MINUS[n], x, last_y:, :]
    pltpu.make_async_copy(moved, moved_hbm, moved_sem).wait()


def fluid(arrived, populations):
    shape = populations.shape
    _, cells_x, cells_y, cells_z = shape
    sources = arrived.shape[0] // 8
    lines = (cells_y + WINDOW) * 24
    face_x = jax.ShapeDtypeStruct((5, cells_y, cells_z), F32)
    face_y = jax.ShapeDtypeStruct((5, cells_x, cells_z), F32)
    vmem = pl.BlockSpec(memory_space=pltpu.VMEM)
    anywhere = pl.BlockSpec(memory_space=pltpu.HBM)
    return pl.pallas_call(
        fluid_kernel,
        out_shape=(
            jax.ShapeDtypeStruct((2, lines + 24, LANES), F32),
            jax.ShapeDtypeStruct((8, LANES), I32),
            jax.ShapeDtypeStruct(shape, F32),
            face_x,
            face_x,
            face_y,
            face_y,
        ),
        in_specs=[vmem, anywhere],
        out_specs=(vmem, vmem, anywhere, vmem, vmem, vmem, vmem),
        scratch_shapes=[
            pltpu.VMEM((7, CAP, sources), F32),
            pltpu.VMEM(shape, F32),
            pltpu.VMEM(shape, F32),
            pltpu.VMEM((UNROLL, cells_z, WIDE), BF16),
            pltpu.VMEM((UNROLL, cells_z, WIDE), BF16),
            pltpu.SMEM((8, LANES), I32),
            pltpu.SemaphoreType.DMA,
            pltpu.SemaphoreType.DMA,
            pltpu.SemaphoreType.DMA,
        ],
        compiler_params=pltpu.CompilerParams(vmem_limit_bytes=54 * MIB),
        cost_estimate=pl.CostEstimate(flops=12 << 30, bytes_accessed=12 << 20, transcendentals=0),
        name="fluid",
    )(arrived, populations)


def gather_kernel(
    arrived_ref, field, spans, vel_ref, arrived, vel_high, vel_low, vel_rows, depth_high, depth_low
):
    chunks = CAP // RANKS
    cells_z = vel_high.shape[2]
    sources = arrived_ref.shape[0] // 8
    for c in range(3, 7):
        arrived[c] = arrived_ref[pl.ds(c, sources, stride=8), :].T
    depth_iota = iota((cells_z, WIDE), 0).astype(F32).astype(BF16)
    span = WINDOW * 24
    lines = vel_high.shape[1]
    for odd in range(2):
        for half in range(2):
            lane = slice(half * LANES, half * LANES + LANES)
            high, low = split(field[half, odd * 24 : odd * 24 + lines, :])
            vel_high[odd, :, lane] = high
            vel_low[odd, :, lane] = low

    def gather_part(depth_parts, weight_x, weight_y, y_first):
        odd = y_first & 1
        at = pl.ds(pl.multiple_of((y_first - odd) * 24, 16), span)
        upper = vel_high[odd, at, :]
        high, low = depth_parts
        total = jnp.dot(
            jnp.concatenate([upper, vel_low[odd, at, :], upper], axis=1),
            jnp.concatenate([high, high, low], axis=0),
            preferred_element_type=F32,
        )
        sums = [None] * 3
        lines = weight_y(y_first)
        for y in range(WINDOW):
            plane = weight_x * lines[y : y + 1, :]
            for c in range(3):
                line = y * 24 + c * 8
                part = plane * total[line : line + 8]
                sums[c] = part if sums[c] is None else sums[c] + part
        out = []
        for c in range(3):
            value = jnp.sum(sums[c], axis=0, keepdims=True)
            out.append(
                jnp.concatenate(
                    [value[:, r * LANES : (r + 1) * LANES] for r in range(RANKS)], axis=0
                )
            )
        return out

    def gather_step(g, carry):
        work = []
        for k in range(UNROLL):
            i = g * UNROLL + k
            rows = chunk_rows(arrived, i, (3, 4, 5, 6))
            high, low = depth_weights(rows, depth_iota)
            depth_high[k] = high
            depth_low[k] = low
            weight_x, weight_y = plane_weights(rows)
            start, number = windows(spans, i)
            at = pl.ds(pl.multiple_of(i * RANKS, RANKS), RANKS)
            values = gather_part((high, low), weight_x, weight_y, start)
            for c in range(3):
                vel_rows[c, at, :] = values[c]
            work.append((k, at, weight_x, weight_y, start, number))
        for k, at, weight_x, weight_y, start, number in work:

            def window_step(
                w, carry, k=k, at=at, weight_x=weight_x, weight_y=weight_y, start=start
            ):
                values = gather_part(
                    (depth_high[k], depth_low[k]), weight_x, weight_y, start + w * WINDOW
                )
                for c in range(3):
                    vel_rows[c, at, :] += values[c]
                return carry

            lax.fori_loop(1, number, window_step, 0)
        return carry

    lax.fori_loop(0, chunks // UNROLL, gather_step, 0)
    for c in range(3):
        vel_ref[pl.ds(c, sources, stride=4), :] = vel_rows[c].T
    vel_ref[pl.ds(3, sources, stride=4), :] = jnp.zeros((sources, CAP), F32)


def gather(arrived, field, spans):
    sources = arrived.shape[0] // 8
    lines = field.shape[1] - 24
    cells_z = 2 * LANES
    vmem = pl.BlockSpec(memory_space=pltpu.VMEM)
    return pl.pallas_call(
        gather_kernel,
        out_shape=jax.ShapeDtypeStruct((4 * sources, CAP), F32),
        in_specs=[vmem, vmem, pl.BlockSpec(memory_space=pltpu.SMEM)],
        out_specs=vmem,
        scratch_shapes=[
            pltpu.VMEM((7, CAP, sources), F32),
            pltpu.VMEM((2, lines, cells_z), BF16),
            pltpu.VMEM((2, lines, cells_z), BF16),
            pltpu.VMEM((3, CAP, sources), F32),
            pltpu.VMEM((UNROLL, cells_z, WIDE), BF16),
            pltpu.VMEM((UNROLL, cells_z, WIDE), BF16),
        ],
        compiler_params=pltpu.CompilerParams(vmem_limit_bytes=54 * MIB),
        cost_estimate=pl.CostEstimate(flops=10 << 30, bytes_accessed=4 << 20, transcendentals=0),
        name="gather",
    )(arrived, field, spans)


def patch_x_kernel(
    moved, x_plus, x_minus, y_plus, y_minus, out, y_plus_out, y_minus_out, write_sem
):
    cells_x, cells_y = out.shape[1:3]
    writes = []
    for faces, qs, x in ((x_plus, X_PLUS, 0), (x_minus, X_MINUS, cells_x - 1)):
        for n, q in enumerate(qs):
            copy = pltpu.make_async_copy(faces.at[n], out.at[q, x], write_sem.at[len(writes)])
            copy.start()
            writes.append(copy)
    y_plus_out[...] = y_plus[...]
    y_minus_out[...] = y_minus[...]
    for faces, qs, x in ((x_plus, X_PLUS, 0), (x_minus, X_MINUS, cells_x - 1)):
        for n, q in enumerate(qs):
            if LATTICE[q, 1] > 0:
                y_plus_out[Y_PLUS.index(q), x : x + 1, :] = faces[n, 0:1, :]
            if LATTICE[q, 1] < 0:
                y_minus_out[Y_MINUS.index(q), x : x + 1, :] = faces[n, cells_y - 1 :, :]
    for copy in writes:
        copy.wait()


def patch_x(moved, x_plus, x_minus, y_plus, y_minus):
    vmem = pl.BlockSpec(memory_space=pltpu.VMEM)
    anywhere = pl.BlockSpec(memory_space=pltpu.HBM)
    face = jax.ShapeDtypeStruct(y_plus.shape, F32)
    return pl.pallas_call(
        patch_x_kernel,
        out_shape=(jax.ShapeDtypeStruct(moved.shape, F32), face, face),
        in_specs=[anywhere, vmem, vmem, vmem, vmem],
        out_specs=(anywhere, vmem, vmem),
        scratch_shapes=[pltpu.SemaphoreType.DMA((10,))],
        input_output_aliases={0: 0},
        compiler_params=pltpu.CompilerParams(vmem_limit_bytes=32 * MIB),
        cost_estimate=pl.CostEstimate(
            flops=0, bytes_accessed=16 * x_plus.size, transcendentals=0
        ),
        name="patch_x",
    )(moved, x_plus, x_minus, y_plus, y_minus)


def patch_y_kernel(moved, y_plus, y_minus, out, done, blocks, read_sem, write_sem):
    done[...] = jnp.zeros_like(done)
    cells_x, cells_y = out.shape[1:3]
    reads = []
    for n, q in enumerate(Y_PLUS + Y_MINUS):
        at = 0 if n < 5 else cells_y - 8
        reads.append(
            pltpu.make_async_copy(out.at[q, :, pl.ds(at, 8), :], blocks.at[n], read_sem.at[n])
        )
        reads[-1].start()
    writes = []
    for n, q in enumerate(Y_PLUS + Y_MINUS):
        reads[n].wait()
        faces, row, at = (y_plus, 0, 0) if n < 5 else (y_minus, 7, cells_y - 8)
        for x in range(cells_x):
            blocks[n, x, row : row + 1, :] = faces[n % 5, x : x + 1, :]
        copy = pltpu.make_async_copy(blocks.at[n], out.at[q, :, pl.ds(at, 8), :], write_sem.at[n])
        copy.start()
        writes.append(copy)
    for copy in writes:
        copy.wait()


def patch_y(moved, y_plus, y_minus):
    _, cells_x, cells_y, cells_z = moved.shape
    vmem = pl.BlockSpec(memory_space=pltpu.VMEM)
    anywhere = pl.BlockSpec(memory_space=pltpu.HBM)
    return pl.pallas_call(
        patch_y_kernel,
        out_shape=(
            jax.ShapeDtypeStruct(moved.shape, F32),
            jax.ShapeDtypeStruct((8, LANES), F32),
        ),
        in_specs=[anywhere, vmem, vmem],
        out_specs=(anywhere, vmem),
        scratch_shapes=[
            pltpu.VMEM((10, cells_x, 8, cells_z), F32),
            pltpu.SemaphoreType.DMA((10,)),
            pltpu.SemaphoreType.DMA((10,)),
        ],
        input_output_aliases={0: 0},
        compiler_params=pltpu.CompilerParams(vmem_limit_bytes=32 * MIB),
        cost_estimate=pl.CostEstimate(
            flops=0, bytes_accessed=80 * cells_x * 8 * cells_z, transcendentals=0
        ),
        name="patch_y",
    )(moved, y_plus, y_minus)


def unpack_kernel(returned, dest_ref, slot_ref, later, out_ref):
    tiles = returned.shape[0] // 4
    rows = dest_ref.shape[0]
    parts = []
    for c in range(3):
        high, low = split(returned[pl.ds(c, tiles, stride=4), :])
        parts.append(jnp.concatenate([high, low], axis=1))
    values = jnp.concatenate(parts, axis=0)
    group = 8
    wide = group * LANES
    for b in range(rows // group):
        slot = jnp.concatenate(
            [slot_ref[b * group + r : b * group + r + 1, :] for r in range(group)], axis=1
        )
        dest = jnp.concatenate(
            [dest_ref[b * group + r : b * group + r + 1, :] for r in range(group)], axis=1
        )
        hot = one_hot(slot == iota((CAP, wide), 0))
        picked = jnp.dot(
            values, jnp.concatenate([hot, hot], axis=0), preferred_element_type=F32
        )
        hit = dest == iota((tiles, wide), 0)
        for c in range(3):
            out_ref[c : c + 1, b * wide : (b + 1) * wide] = jnp.sum(
                jnp.where(hit, picked[c * tiles : (c + 1) * tiles, :], 0.0), axis=0, keepdims=True
            )


def unpack(returned, dest, slot, later):
    count = dest.size
    return pl.pallas_call(
        unpack_kernel,
        out_shape=jax.ShapeDtypeStruct((3, count), F32),
        in_specs=[pl.BlockSpec(memory_space=pltpu.VMEM)] * 4,
        out_specs=pl.BlockSpec(memory_space=pltpu.VMEM),
        compiler_params=pltpu.CompilerParams(vmem_limit_bytes=40 * MIB),
        name="unpack",
    )(returned, dest, slot, later)


def to_all(rows, tiles):
    blocks = rows.reshape(tiles, -1, CAP)
    blocks = lax.all_to_all(blocks, ("gx", "gy"), split_axis=0, concat_axis=0, tiled=True)
    return blocks.reshape(-1, CAP)


def both_ways(axis, low, high):
    size = lax.axis_size(axis)
    forward = [(i, (i + 1) % size) for i in range(size)]
    backward = [(target, source) for source, target in forward]
    return lax.ppermute(low, axis, forward), lax.ppermute(high, axis, backward)


def shards(populations, displacement, offsets, cell_local, destination, triangles, stiffness):
    tiles = lax.axis_size("gx") * lax.axis_size("gy")
    dest_rows = destination.reshape(-1, LANES)
    packed, slot = sender(
        displacement,
        offsets,
        cell_local,
        dest_rows,
        triangles.T,
        stiffness.reshape(-1, LANES),
        tiles,
    )
    arrived = to_all(packed, tiles)
    field, spans, moved, x_plus, x_minus, y_plus, y_minus = fluid(arrived, populations)
    slot_velocity = gather(arrived, field, spans)
    returned = to_all(slot_velocity, tiles)
    x_plus, x_minus = both_ways("gx", x_plus, x_minus)
    moved, y_plus, y_minus = patch_x(moved, x_plus, x_minus, y_plus, y_minus)
    y_plus, y_minus = both_ways("gy", y_plus, y_minus)
    populations_next, done = patch_y(moved, y_plus, y_minus)
    marker_velocity = unpack(returned, dest_rows, slot, done)
    return (populations_next, marker_velocity)


def solution(mesh):
    return jax.shard_map(
        shards,
        mesh=mesh,
        in_specs=(
            P(None, "gx", "gy", None),
            P(None, ("gx", "gy")),
            P(None, ("gx", "gy")),
            P(None, ("gx", "gy")),
            P(("gx", "gy"), None),
            P(("gx", "gy"), None),
            P(("gx", "gy")),
        ),
        out_specs=(P(None, "gx", "gy", None), P(None, ("gx", "gy"))),
        check_vma=False,
    )
```

```python
import jax
import jax.numpy as jnp
import numpy as np
from jax import lax
from jax.experimental import pallas as pl
from jax.experimental.pallas import tpu as pltpu
from jax.sharding import PartitionSpec as P

CAP = 128
LANES = 128
WINDOW = 12
RANKS = 8
WIDE = RANKS * LANES
UNROLL = 8

LATTICE = np.array(
    [
        [0, 0, 0],
        [1, 0, 0],
        [-1, 0, 0],
        [0, 1, 0],
        [0, -1, 0],
        [0, 0, 1],
        [0, 0, -1],
        [1, 1, 0],
        [-1, -1, 0],
        [1, -1, 0],
        [-1, 1, 0],
        [1, 0, 1],
        [-1, 0, -1],
        [1, 0, -1],
        [-1, 0, 1],
        [0, 1, 1],
        [0, -1, -1],
        [0, 1, -1],
        [0, -1, 1],
    ]
)
LATTICE_WEIGHTS = [1.0 / 3.0] + [1.0 / 18.0] * 6 + [1.0 / 36.0] * 12
RELAX = 0.8
X_PLUS = [q for q in range(19) if LATTICE[q, 0] == 1]
X_MINUS = [q for q in range(19) if LATTICE[q, 0] == -1]
Y_PLUS = [q for q in range(19) if LATTICE[q, 1] == 1]
Y_MINUS = [q for q in range(19) if LATTICE[q, 1] == -1]
DIAGONAL = [q for q in range(19) if LATTICE[q, 0] != 0 and LATTICE[q, 1] != 0]
NT = (((1,), (1,)), ((), ()))
F32 = jnp.float32
BF16 = jnp.bfloat16
I32 = jnp.int32
MIB = 1 << 20


def iota(shape, dim):
    return lax.broadcasted_iota(I32, shape, dim)


def split(value):
    high = value.astype(BF16)
    low = (value - high.astype(F32)).astype(BF16)
    return high, low


def one_hot(hit):
    return jnp.where(hit, 1.0, 0.0).astype(BF16)


def lane_pick(row, lanes):
    return jnp.take_along_axis(jnp.broadcast_to(row, lanes.shape), lanes, axis=1)


def sender_kernel(
    disp_hbm,
    offs_hbm,
    cell_hbm,
    dest_hbm,
    tri_hbm,
    stiff_hbm,
    packed_ref,
    slot_ref,
    disp_ref,
    offs_ref,
    cell_ref,
    dest_ref,
    tri_ref,
    stiff_ref,
    disp_rows,
    pay,
    tri_rows,
    term_high,
    term_low,
    acc,
    order,
    place,
    sorted_dest,
    sorted_slot,
    mask,
    sems,
):
    fetches = []
    for n, (source, target) in enumerate(
        (
            (cell_hbm, cell_ref),
            (dest_hbm, dest_ref),
            (tri_hbm, tri_ref),
            (disp_hbm, disp_ref),
            (stiff_hbm, stiff_ref),
            (offs_hbm, offs_ref),
        )
    ):
        fetches.append(pltpu.make_async_copy(source, target, sems.at[n]))
        fetches[-1].start()
    count = disp_ref.shape[1]
    rows = count // LANES
    tri_rows_count = tri_ref.shape[1] // LANES
    tiles = packed_ref.shape[0] // 8
    width = 256
    blocks = count // width
    bins = 32
    for fetch in fetches:
        fetch.wait()
    for r in range(rows):
        lane = pl.ds(r * LANES, LANES)
        flat = (cell_ref[0:1, lane] * 32 + cell_ref[1:2, lane]) * 256 + cell_ref[2:3, lane]
        pay[6, r : r + 1, :] = flat.astype(F32)
        for c in range(3):
            disp_rows[c, r : r + 1, :] = disp_ref[c : c + 1, lane]
            pay[3 + c, r : r + 1, :] = offs_ref[c : c + 1, lane]
    for r in range(tri_rows_count):
        for v in range(3):
            tri_rows[v, r : r + 1, :] = tri_ref[v : v + 1, pl.ds(r * LANES, LANES)]

    earlier = one_hot(iota((width, 2 * width), 0) < iota((width, 2 * width), 1))
    bin_iota = iota((bins, width), 0)
    y_hits = [cell_ref[1:2, b * width : (b + 1) * width] == bin_iota for b in range(blocks)]
    y_counts = jnp.dot(
        jnp.concatenate([one_hot(hit) for hit in y_hits], axis=0),
        earlier,
        preferred_element_type=F32,
    )
    totals = y_counts[0:bins, width:]
    for b in range(1, blocks):
        totals = totals + y_counts[b * bins : (b + 1) * bins, width:]
    below = jnp.where(iota((bins, bins), 1) < iota((bins, bins), 0), 1.0, 0.0)
    first = jnp.dot(below, totals, preferred_element_type=F32, precision=lax.Precision.HIGHEST)
    within = iota((1, width), 1).astype(F32)
    running = first
    left = []
    right = []
    for b in range(blocks):
        own = y_counts[b * bins : (b + 1) * bins, 0:width] + running
        running = running + y_counts[b * bins : (b + 1) * bins, width:]
        at = jnp.sum(jnp.where(y_hits[b], own, 0.0), axis=0, keepdims=True).astype(I32)
        place[2 * b : 2 * b + 1, :] = at[:, 0:LANES]
        place[2 * b + 1 : 2 * b + 2, :] = at[:, LANES:]
        hit = (at >> 7) == iota((rows, width), 0)
        left.append(
            jnp.concatenate(
                [
                    jnp.where(hit, within, 0.0).astype(BF16),
                    jnp.where(hit, float(b), 0.0).astype(BF16),
                ],
                axis=0,
            )
        )
        right.append(one_hot((at & (LANES - 1)) == iota((LANES, width), 0)))
    order[...] = lax.dot_general(
        jnp.concatenate(left, axis=1),
        jnp.concatenate(right, axis=1),
        NT,
        preferred_element_type=F32,
    )
    for i in range(rows // 8):
        block = slice(8 * i, 8 * i + 8)
        marker = (order[rows + 8 * i : rows + 8 * i + 8, :] * 256.0 + order[block, :]).astype(I32)
        low = marker & (LANES - 1)
        high = marker >> 7
        found = jnp.zeros((8, LANES), I32)
        for r in range(rows):
            found = jnp.where(high == r, lane_pick(dest_ref[r : r + 1, :], low), found)
        sorted_dest[block, :] = found

    def row_of(ref, b, at=0):
        return jnp.concatenate(
            [ref[at + 2 * b : at + 2 * b + 1, :], ref[at + 2 * b + 1 : at + 2 * b + 2, :]], axis=1
        )

    tile_iota = iota((tiles, width), 0)
    hots = []
    cums = []
    for b in range(blocks):
        mask[:, b * width : (b + 1) * width] = one_hot(row_of(sorted_dest, b) == tile_iota)
        at = within + float(b * width)
        hots.append((at >= first) & (at < first + totals))
        cums.append(one_hot(at < first))
    before = jnp.dot(
        jnp.concatenate([mask[:, b * width : (b + 1) * width] for b in range(blocks)], axis=0),
        earlier,
        preferred_element_type=F32,
    )
    smaller = lax.dot_general(
        jnp.concatenate(cums, axis=1), mask[...], NT, preferred_element_type=F32
    )
    room = float(CAP) - smaller[bins - 1 : bins, :]
    ahead = jnp.zeros((1, tiles), F32)
    shift = []
    for y in range(bins):
        ahead = jnp.maximum(ahead, float((y * CAP) // (bins - 1)) - smaller[y : y + 1, :])
        shift.append(jnp.minimum(ahead, room))
    shift = jnp.concatenate(shift, axis=0).astype(BF16)
    shifts = jnp.dot(shift, mask[...], preferred_element_type=F32)
    running = jnp.zeros((tiles, width), F32)
    left = []
    right = []
    for b in range(blocks):
        lane = slice(b * width, (b + 1) * width)
        hit = row_of(sorted_dest, b) == tile_iota
        own = before[b * tiles : (b + 1) * tiles, 0:width] + running
        running = running + before[b * tiles : (b + 1) * tiles, width:]
        slot = jnp.sum(jnp.where(hit, own, 0.0), axis=0, keepdims=True) + jnp.sum(
            jnp.where(hots[b], shifts[:, lane], 0.0), axis=0, keepdims=True
        )
        slot = slot.astype(I32)
        sorted_slot[2 * b : 2 * b + 1, :] = slot[:, 0:LANES]
        sorted_slot[2 * b + 1 : 2 * b + 2, :] = slot[:, LANES:]
        left.append(
            jnp.concatenate(
                [
                    jnp.where(hit, row_of(order, b), 0.0).astype(BF16),
                    jnp.where(hit, row_of(order, b, rows) + 1.0, 0.0).astype(BF16),
                ],
                axis=0,
            )
        )
        right.append(one_hot(slot == iota((CAP, width), 0)))
    inverse = lax.dot_general(
        jnp.concatenate(left, axis=1),
        jnp.concatenate(right, axis=1),
        NT,
        preferred_element_type=F32,
    )
    for i in range(rows // 8):
        block = slice(8 * i, 8 * i + 8)
        at = place[block, :]
        low = at & (LANES - 1)
        high = at >> 7
        found = jnp.zeros((8, LANES), I32)
        for r in range(rows):
            found = jnp.where(high == r, lane_pick(sorted_slot[r : r + 1, :], low), found)
        slot_ref[block, :] = found

    def gather_step(i, carry):
        block = pl.ds(i * 8, 8)
        corner = []
        for v in range(3):
            index = tri_rows[v, block, :]
            low = index & (LANES - 1)
            high = index >> 7
            found = [jnp.zeros((8, LANES), F32) for _ in range(3)]
            for r in range(rows):
                hit = high == r
                for c in range(3):
                    found[c] = jnp.where(hit, lane_pick(disp_rows[c, r : r + 1, :], low), found[c])
            corner.append(found)
        stiff = stiff_ref[block, :]
        for c in range(3):
            total = corner[0][c] + corner[1][c] + corner[2][c]
            for v in range(3):
                term = stiff * (total - 3.0 * corner[v][c])
                rounded = term.astype(BF16).astype(F32)
                term_high[v, c, block, :] = rounded
                term_low[v, c, block, :] = term - rounded
        return carry

    for i in range(tri_rows_count // 8):
        gather_step(i, 0)

    acc[...] = jnp.zeros_like(acc)
    row_iota = iota((rows, LANES), 0)
    lane_iota = iota((LANES, LANES), 0)
    step_rows = 32
    for v in range(3):

        def scatter_step(i, carry, v=v):
            left = []
            right = []
            for k in range(step_rows):
                at = pl.ds(i * step_rows + k, 1)
                index = tri_rows[v, at, :]
                hit = row_iota == (index >> 7)
                parts = []
                for c in range(3):
                    parts.append(jnp.where(hit, term_high[v, c, at, :], 0.0).astype(BF16))
                    parts.append(jnp.where(hit, term_low[v, c, at, :], 0.0).astype(BF16))
                left.append(jnp.concatenate(parts, axis=0))
                right.append(one_hot(lane_iota == (index & (LANES - 1))))
            acc[...] += lax.dot_general(
                jnp.concatenate(left, axis=1),
                jnp.concatenate(right, axis=1),
                NT,
                preferred_element_type=F32,
            )
            return carry

        for i in range(tri_rows_count // step_rows):
            scatter_step(i, 0)
    for c in range(3):
        at = c * 2 * rows
        pay[c] = acc[at : at + rows, :] + acc[at + rows : at + 2 * rows, :]

    for i in range(tiles // 8):
        block = slice(8 * i, 8 * i + 8)
        group = inverse[tiles + 8 * i : tiles + 8 * i + 8, :]
        valid = group > 0.5
        marker = ((group - 1.0) * 256.0 + inverse[block, :]).astype(I32)
        marker = jnp.maximum(marker, 0)
        low = marker & (LANES - 1)
        high = marker >> 7
        found = [jnp.zeros((8, LANES), F32) for _ in range(7)]
        for r in range(rows):
            hit = high == r
            for c in range(7):
                found[c] = jnp.where(hit, lane_pick(pay[c, r : r + 1, :], low), found[c])
        for c in range(7):
            value = jnp.where(valid, found[c], -1.0 if c == 6 else 0.0)
            packed_ref[pl.ds(64 * i + c, 8, stride=8), :] = value
        packed_ref[pl.ds(64 * i + 7, 8, stride=8), :] = jnp.zeros((8, LANES), F32)


def sender(displacement, offsets, cell_local, destination, triangles, stiffness, tiles):
    count = displacement.shape[1]
    tris = triangles.shape[1]
    rows = count // LANES
    return pl.pallas_call(
        sender_kernel,
        out_shape=(
            jax.ShapeDtypeStruct((8 * tiles, CAP), F32),
            jax.ShapeDtypeStruct((rows, LANES), I32),
        ),
        in_specs=[pl.BlockSpec(memory_space=pltpu.HBM)] * 6,
        out_specs=(pl.BlockSpec(memory_space=pltpu.VMEM),) * 2,
        scratch_shapes=[
            pltpu.VMEM(displacement.shape, F32),
            pltpu.VMEM(offsets.shape, F32),
            pltpu.VMEM(cell_local.shape, I32),
            pltpu.VMEM(destination.shape, I32),
            pltpu.VMEM(triangles.shape, I32),
            pltpu.VMEM(stiffness.shape, F32),
            pltpu.VMEM((3, rows, LANES), F32),
            pltpu.VMEM((7, rows, LANES), F32),
            pltpu.VMEM((3, tris // LANES, LANES), I32),
            pltpu.VMEM((3, 3, tris // LANES, LANES), F32),
            pltpu.VMEM((3, 3, tris // LANES, LANES), F32),
            pltpu.VMEM((6 * rows, LANES), F32),
            pltpu.VMEM((2 * rows, LANES), F32),
            pltpu.VMEM((rows, LANES), I32),
            pltpu.VMEM((rows, LANES), I32),
            pltpu.VMEM((rows, LANES), I32),
            pltpu.VMEM((tiles, count), BF16),
            pltpu.SemaphoreType.DMA((6,)),
        ],
        compiler_params=pltpu.CompilerParams(vmem_limit_bytes=60 * MIB),
        cost_estimate=pl.CostEstimate(flops=4 << 30, bytes_accessed=1 << 20, transcendentals=0),
        name="sender",
    )(displacement, offsets, cell_local, destination, triangles, stiffness)


def chunk_rows(arrived, i, channels):
    out = {}
    for c in channels:
        tile = arrived[c, pl.ds(pl.multiple_of(i * RANKS, RANKS), RANKS), :]
        out[c] = jnp.concatenate([tile[r : r + 1, :] for r in range(RANKS)], axis=1)
    return out


def plane_weights(rows):
    cell = rows[6].astype(I32)
    y = (cell >> 8) & 31
    x = cell >> 13
    eight = iota((8, WIDE), 0)
    weight_x = jnp.where(eight == x, 1.0 - rows[3], jnp.where(eight == x + 1, rows[3], 0.0))

    def weight_y(first):
        line = iota((16, WIDE), 0) + first
        return jnp.where(y == line, 1.0 - rows[4], jnp.where(y + 1 == line, rows[4], 0.0))

    return weight_x, weight_y


def depth_weights(rows, depth_iota):
    depth = rows[6].astype(I32) & 255
    first = depth_iota == depth.astype(F32).astype(BF16)
    second = depth_iota == (depth + 1).astype(F32).astype(BF16)
    lower_high, lower_low = split(1.0 - rows[5])
    upper_high, upper_low = split(rows[5])
    none = jnp.zeros((), BF16)
    high = jnp.where(first, lower_high, jnp.where(second, upper_high, none))
    low = jnp.where(first, lower_low, jnp.where(second, upper_low, none))
    return high, low


def windows(spans, i):
    start = jnp.minimum(spans[0, i * RANKS], 31)
    end = 2 - spans[1, i * RANKS]
    return start, jnp.maximum(end - start + WINDOW - 1, 0) // WINDOW


def signed(sign, value):
    return value if sign > 0 else -value


def plus(total, sign, value):
    if total is None:
        return signed(sign, value)
    return total + value if sign > 0 else total - value


def fluid_kernel(
    arrived_ref,
    pops_hbm,
    field,
    span_rows,
    moved_hbm,
    x_plus,
    x_minus,
    y_plus,
    y_minus,
    arrived,
    pops,
    moved,
    depth_high,
    depth_low,
    spans,
    pops_sem,
    span_sem,
    moved_sem,
):
    fetch = pltpu.make_async_copy(pops_hbm, pops, pops_sem)
    fetch.start()
    chunks = CAP // RANKS
    cells_x, cells_y, cells_z = moved.shape[1:]
    sources = arrived_ref.shape[0] // 8
    for c in range(7):
        arrived[c] = arrived_ref[pl.ds(c, sources, stride=8), :].T

    cell = arrived_ref[pl.ds(6, sources, stride=8), :].astype(I32)
    y_all = (cell >> 8) & 31
    lowest = jnp.min(jnp.where(cell < 0, 99, y_all), axis=0, keepdims=True)
    highest = jnp.max(jnp.where(cell < 0, -99, y_all), axis=0, keepdims=True)
    extent = jnp.broadcast_to(lowest, (8, LANES))
    extent = jnp.where(iota((8, LANES), 0) == 1, -highest, extent)
    for step in (1, 2, 4):
        extent = jnp.minimum(extent, pltpu.roll(extent, LANES - step, 1))
    span_rows[...] = extent
    share = pltpu.make_async_copy(span_rows, spans, span_sem)
    share.start()
    field[...] = jnp.zeros_like(field)
    depth_iota = iota((cells_z, WIDE), 0).astype(F32).astype(BF16)
    span = WINDOW * 24
    share.wait()

    def spread_part(rows, depth_parts, pushed, weight_y, y_first):
        parts = []
        lines = weight_y(y_first)
        for y in range(WINDOW):
            at_y = lines[y : y + 1, :]
            for c in range(3):
                parts.append(pushed[c] * at_y)
        spread_high, spread_low = split(jnp.concatenate(parts, axis=0))
        high, low = depth_parts
        add = lax.dot_general(
            jnp.concatenate([spread_high, spread_low, spread_high], axis=1),
            jnp.concatenate([high, high, low], axis=1),
            NT,
            preferred_element_type=F32,
        )
        at = pl.ds(pl.multiple_of(y_first * 24, 8), span)
        field[0, at, :] += add[:, 0:LANES]
        field[1, at, :] += add[:, LANES:]

    def spread_step(g, carry):
        work = []
        for k in range(UNROLL):
            i = g * UNROLL + k
            rows = chunk_rows(arrived, i, range(7))
            high, low = depth_weights(rows, depth_iota)
            depth_high[k] = high
            depth_low[k] = low
            weight_x, weight_y = plane_weights(rows)
            pushed = [weight_x * rows[c] for c in range(3)]
            start, number = windows(spans, i)
            spread_part(rows, (high, low), pushed, weight_y, start)
            work.append((k, rows, pushed, weight_y, start, number))
        for k, rows, pushed, weight_y, start, number in work:

            def window_step(w, carry, k=k, rows=rows, pushed=pushed, weight_y=weight_y, start=start):
                spread_part(
                    rows, (depth_high[k], depth_low[k]), pushed, weight_y, start + w * WINDOW
                )
                return carry

            lax.fori_loop(1, number, window_step, 0)
        return carry

    lax.fori_loop(0, chunks // UNROLL, spread_step, 0)

    fetch.wait()
    push = 1.0 - 0.5 / RELAX
    rest = 1.0 - 1.0 / RELAX

    def plane_step(x, carry):
        rho = pops[0, x]
        for q in range(1, 19):
            rho = rho + pops[q, x]
        inverse = 1.0 / rho
        pull = []
        velocity = []
        for c in range(3):
            moment = None
            for q in range(19):
                if LATTICE[q, c] != 0:
                    moment = plus(moment, LATTICE[q, c], pops[q, x])
            at = pl.ds(c * 8 + x, cells_y, stride=24)
            force = jnp.concatenate([field[0, at, :], field[1, at, :]], axis=1)
            flow = (moment + 0.5 * force) * inverse
            field[0, at, :] = flow[:, 0:LANES]
            field[1, at, :] = flow[:, LANES:]
            pull.append(force)
            velocity.append(flow)
        usq = velocity[0] * velocity[0] + velocity[1] * velocity[1] + velocity[2] * velocity[2]
        udotf = velocity[0] * pull[0] + velocity[1] * pull[1] + velocity[2] * pull[2]
        base = rho * (1.0 - 1.5 * usq) * (1.0 / RELAX) - (3.0 * push) * udotf

        def emit(q, value):
            cx, cy, cz = (int(v) for v in LATTICE[q])
            if cy != 0:
                value = pltpu.roll(value, cy % cells_y, 0)
            if cz != 0:
                value = pltpu.roll(value, cz % cells_z, 1)
            to = x + cx
            if cx > 0:
                to = jnp.where(to == cells_x, 0, to)
            if cx < 0:
                to = jnp.where(to < 0, cells_x - 1, to)
            moved[q, to] = value
            pltpu.make_async_copy(moved.at[q, to], moved_hbm.at[q, to], moved_sem).start()

        emit(0, rest * pops[0, x] + LATTICE_WEIGHTS[0] * base)
        for q in range(1, 19, 2):
            along = None
            pulled = None
            for c in range(3):
                if LATTICE[q, c] != 0:
                    along = plus(along, LATTICE[q, c], velocity[c])
                    pulled = plus(pulled, LATTICE[q, c], pull[c])
            odd = (3.0 / RELAX) * rho * along + (3.0 * push) * pulled
            even = base + along * ((4.5 / RELAX) * rho * along + (9.0 * push) * pulled)
            weight = LATTICE_WEIGHTS[q]
            emit(q, rest * pops[q, x] + weight * (even + odd))
            emit(q + 1, rest * pops[q + 1, x] + weight * (even - odd))
        return carry

    lax.fori_loop(0, cells_x, plane_step, 0)
    last_x = cells_x - 1
    last_y = cells_y - 1
    for n in range(5):
        x_plus[n] = moved[X_PLUS[n], 0]
        x_minus[n] = moved[X_MINUS[n], last_x]
        for x in range(cells_x):
            y_plus[n, x : x + 1, :] = moved[Y_PLUS[n], x, 0:1, :]
            y_minus[n, x : x + 1, :] = moved[Y_MINUS[n], x, last_y:, :]
    pltpu.make_async_copy(moved, moved_hbm, moved_sem).wait()


def fluid(arrived, populations):
    shape = populations.shape
    _, cells_x, cells_y, cells_z = shape
    sources = arrived.shape[0] // 8
    lines = (cells_y + WINDOW) * 24
    face_x = jax.ShapeDtypeStruct((5, cells_y, cells_z), F32)
    face_y = jax.ShapeDtypeStruct((5, cells_x, cells_z), F32)
    vmem = pl.BlockSpec(memory_space=pltpu.VMEM)
    anywhere = pl.BlockSpec(memory_space=pltpu.HBM)
    return pl.pallas_call(
        fluid_kernel,
        out_shape=(
            jax.ShapeDtypeStruct((2, lines + 24, LANES), F32),
            jax.ShapeDtypeStruct((8, LANES), I32),
            jax.ShapeDtypeStruct(shape, F32),
            face_x,
            face_x,
            face_y,
            face_y,
        ),
        in_specs=[vmem, anywhere],
        out_specs=(vmem, vmem, anywhere, vmem, vmem, vmem, vmem),
        scratch_shapes=[
            pltpu.VMEM((7, CAP, sources), F32),
            pltpu.VMEM(shape, F32),
            pltpu.VMEM(shape, F32),
            pltpu.VMEM((UNROLL, cells_z, WIDE), BF16),
            pltpu.VMEM((UNROLL, cells_z, WIDE), BF16),
            pltpu.SMEM((8, LANES), I32),
            pltpu.SemaphoreType.DMA,
            pltpu.SemaphoreType.DMA,
            pltpu.SemaphoreType.DMA,
        ],
        compiler_params=pltpu.CompilerParams(vmem_limit_bytes=50 * MIB),
        cost_estimate=pl.CostEstimate(flops=12 << 30, bytes_accessed=12 << 20, transcendentals=0),
        name="fluid",
    )(arrived, populations)


def gather_kernel(
    arrived_ref, field, spans, vel_ref, arrived, vel_high, vel_low, vel_rows, depth_high, depth_low
):
    chunks = CAP // RANKS
    cells_z = vel_high.shape[2]
    sources = arrived_ref.shape[0] // 8
    for c in range(3, 7):
        arrived[c] = arrived_ref[pl.ds(c, sources, stride=8), :].T
    depth_iota = iota((cells_z, WIDE), 0).astype(F32).astype(BF16)
    span = WINDOW * 24
    lines = vel_high.shape[1]
    for odd in range(2):
        for half in range(2):
            lane = slice(half * LANES, half * LANES + LANES)
            high, low = split(field[half, odd * 24 : odd * 24 + lines, :])
            vel_high[odd, :, lane] = high
            vel_low[odd, :, lane] = low

    def gather_part(depth_parts, weight_x, weight_y, y_first):
        odd = y_first & 1
        at = pl.ds(pl.multiple_of((y_first - odd) * 24, 16), span)
        upper = vel_high[odd, at, :]
        high, low = depth_parts
        total = jnp.dot(
            jnp.concatenate([upper, vel_low[odd, at, :], upper], axis=1),
            jnp.concatenate([high, high, low], axis=0),
            preferred_element_type=F32,
        )
        sums = [None] * 3
        lines = weight_y(y_first)
        for y in range(WINDOW):
            plane = weight_x * lines[y : y + 1, :]
            for c in range(3):
                line = y * 24 + c * 8
                part = plane * total[line : line + 8]
                sums[c] = part if sums[c] is None else sums[c] + part
        out = []
        for c in range(3):
            value = jnp.sum(sums[c], axis=0, keepdims=True)
            out.append(
                jnp.concatenate(
                    [value[:, r * LANES : (r + 1) * LANES] for r in range(RANKS)], axis=0
                )
            )
        return out

    def gather_step(g, carry):
        work = []
        for k in range(UNROLL):
            i = g * UNROLL + k
            rows = chunk_rows(arrived, i, (3, 4, 5, 6))
            high, low = depth_weights(rows, depth_iota)
            depth_high[k] = high
            depth_low[k] = low
            weight_x, weight_y = plane_weights(rows)
            start, number = windows(spans, i)
            at = pl.ds(pl.multiple_of(i * RANKS, RANKS), RANKS)
            values = gather_part((high, low), weight_x, weight_y, start)
            for c in range(3):
                vel_rows[c, at, :] = values[c]
            work.append((k, at, weight_x, weight_y, start, number))
        for k, at, weight_x, weight_y, start, number in work:

            def window_step(
                w, carry, k=k, at=at, weight_x=weight_x, weight_y=weight_y, start=start
            ):
                values = gather_part(
                    (depth_high[k], depth_low[k]), weight_x, weight_y, start + w * WINDOW
                )
                for c in range(3):
                    vel_rows[c, at, :] += values[c]
                return carry

            lax.fori_loop(1, number, window_step, 0)
        return carry

    lax.fori_loop(0, chunks // UNROLL, gather_step, 0)
    for c in range(3):
        vel_ref[pl.ds(c, sources, stride=4), :] = vel_rows[c].T
    vel_ref[pl.ds(3, sources, stride=4), :] = jnp.zeros((sources, CAP), F32)


def gather(arrived, field, spans):
    sources = arrived.shape[0] // 8
    lines = field.shape[1] - 24
    cells_z = 2 * LANES
    vmem = pl.BlockSpec(memory_space=pltpu.VMEM)
    return pl.pallas_call(
        gather_kernel,
        out_shape=jax.ShapeDtypeStruct((4 * sources, CAP), F32),
        in_specs=[vmem, vmem, pl.BlockSpec(memory_space=pltpu.SMEM)],
        out_specs=vmem,
        scratch_shapes=[
            pltpu.VMEM((7, CAP, sources), F32),
            pltpu.VMEM((2, lines, cells_z), BF16),
            pltpu.VMEM((2, lines, cells_z), BF16),
            pltpu.VMEM((3, CAP, sources), F32),
            pltpu.VMEM((UNROLL, cells_z, WIDE), BF16),
            pltpu.VMEM((UNROLL, cells_z, WIDE), BF16),
        ],
        compiler_params=pltpu.CompilerParams(vmem_limit_bytes=36 * MIB),
        cost_estimate=pl.CostEstimate(flops=10 << 30, bytes_accessed=4 << 20, transcendentals=0),
        name="gather",
    )(arrived, field, spans)


def patch_x_kernel(
    moved,
    x_plus,
    x_minus,
    y_plus,
    y_minus,
    sums,
    out,
    y_plus_out,
    y_minus_out,
    sums_out,
    write_sem,
):
    cells_x, cells_y = out.shape[1:3]
    writes = []
    for faces, qs, x in ((x_plus, X_PLUS, 0), (x_minus, X_MINUS, cells_x - 1)):
        for n, q in enumerate(qs):
            copy = pltpu.make_async_copy(faces.at[n], out.at[q, x], write_sem.at[len(writes)])
            copy.start()
            writes.append(copy)
    y_plus_out[...] = y_plus[...]
    y_minus_out[...] = y_minus[...]
    for faces, qs, x in ((x_plus, X_PLUS, 0), (x_minus, X_MINUS, cells_x - 1)):
        for n, q in enumerate(qs):
            if LATTICE[q, 1] > 0:
                y_plus_out[Y_PLUS.index(q), x : x + 1, :] = faces[n, 0:1, :]
            if LATTICE[q, 1] < 0:
                y_minus_out[Y_MINUS.index(q), x : x + 1, :] = faces[n, cells_y - 1 :, :]
    for copy in writes:
        copy.wait()


def patch_x(moved, x_plus, x_minus, y_plus, y_minus, sums):
    vmem = pl.BlockSpec(memory_space=pltpu.VMEM)
    anywhere = pl.BlockSpec(memory_space=pltpu.HBM)
    face = jax.ShapeDtypeStruct(y_plus.shape, F32)
    return pl.pallas_call(
        patch_x_kernel,
        out_shape=(
            jax.ShapeDtypeStruct(moved.shape, F32),
            face,
            face,
            jax.ShapeDtypeStruct(sums.shape, F32),
        ),
        in_specs=[anywhere, vmem, vmem, vmem, vmem, anywhere],
        out_specs=(anywhere, vmem, vmem, anywhere),
        scratch_shapes=[pltpu.SemaphoreType.DMA((10,))],
        input_output_aliases={0: 0, 5: 3},
        compiler_params=pltpu.CompilerParams(vmem_limit_bytes=32 * MIB),
        cost_estimate=pl.CostEstimate(
            flops=0, bytes_accessed=16 * x_plus.size, transcendentals=0
        ),
        name="patch_x",
    )(moved, x_plus, x_minus, y_plus, y_minus, sums)


def patch_y_kernel(moved, y_plus, y_minus, out, done, blocks, read_sem, write_sem):
    done[...] = jnp.zeros_like(done)
    cells_x, cells_y = out.shape[1:3]
    reads = []
    for n, q in enumerate(Y_PLUS + Y_MINUS):
        at = 0 if n < 5 else cells_y - 8
        reads.append(
            pltpu.make_async_copy(out.at[q, :, pl.ds(at, 8), :], blocks.at[n], read_sem.at[n])
        )
        reads[-1].start()
    writes = []
    for n, q in enumerate(Y_PLUS + Y_MINUS):
        reads[n].wait()
        faces, row, at = (y_plus, 0, 0) if n < 5 else (y_minus, 7, cells_y - 8)
        for x in range(cells_x):
            blocks[n, x, row : row + 1, :] = faces[n % 5, x : x + 1, :]
        copy = pltpu.make_async_copy(blocks.at[n], out.at[q, :, pl.ds(at, 8), :], write_sem.at[n])
        copy.start()
        writes.append(copy)
    for copy in writes:
        copy.wait()


def patch_y(moved, y_plus, y_minus):
    _, cells_x, cells_y, cells_z = moved.shape
    vmem = pl.BlockSpec(memory_space=pltpu.VMEM)
    anywhere = pl.BlockSpec(memory_space=pltpu.HBM)
    return pl.pallas_call(
        patch_y_kernel,
        out_shape=(
            jax.ShapeDtypeStruct(moved.shape, F32),
            jax.ShapeDtypeStruct((8, LANES), F32),
        ),
        in_specs=[anywhere, vmem, vmem],
        out_specs=(anywhere, vmem),
        scratch_shapes=[
            pltpu.VMEM((10, cells_x, 8, cells_z), F32),
            pltpu.SemaphoreType.DMA((10,)),
            pltpu.SemaphoreType.DMA((10,)),
        ],
        input_output_aliases={0: 0},
        compiler_params=pltpu.CompilerParams(vmem_limit_bytes=32 * MIB),
        cost_estimate=pl.CostEstimate(
            flops=0, bytes_accessed=80 * cells_x * 8 * cells_z, transcendentals=0
        ),
        name="patch_y",
    )(moved, y_plus, y_minus)


def unpack_kernel(returned, dest_ref, slot_ref, later, out_ref):
    tiles = returned.shape[0] // 4
    rows = dest_ref.shape[0]
    parts = []
    for c in range(3):
        high, low = split(returned[pl.ds(c, tiles, stride=4), :])
        parts.append(jnp.concatenate([high, low], axis=1))
    values = jnp.concatenate(parts, axis=0)
    group = 8
    wide = group * LANES
    for b in range(rows // group):
        slot = jnp.concatenate(
            [slot_ref[b * group + r : b * group + r + 1, :] for r in range(group)], axis=1
        )
        dest = jnp.concatenate(
            [dest_ref[b * group + r : b * group + r + 1, :] for r in range(group)], axis=1
        )
        hot = one_hot(slot == iota((CAP, wide), 0))
        picked = jnp.dot(
            values, jnp.concatenate([hot, hot], axis=0), preferred_element_type=F32
        )
        hit = dest == iota((tiles, wide), 0)
        for c in range(3):
            out_ref[c : c + 1, b * wide : (b + 1) * wide] = jnp.sum(
                jnp.where(hit, picked[c * tiles : (c + 1) * tiles, :], 0.0), axis=0, keepdims=True
            )


def unpack(returned, dest, slot, later):
    count = dest.size
    return pl.pallas_call(
        unpack_kernel,
        out_shape=jax.ShapeDtypeStruct((3, count), F32),
        in_specs=[pl.BlockSpec(memory_space=pltpu.VMEM)] * 4,
        out_specs=pl.BlockSpec(memory_space=pltpu.VMEM),
        compiler_params=pltpu.CompilerParams(vmem_limit_bytes=32 * MIB),
        name="unpack",
    )(returned, dest, slot, later)


def to_all(rows, tiles):
    blocks = rows.reshape(tiles, -1, CAP)
    blocks = lax.all_to_all(blocks, ("gx", "gy"), split_axis=0, concat_axis=0, tiled=True)
    return blocks.reshape(-1, CAP)


def both_ways(axis, low, high):
    size = lax.axis_size(axis)
    forward = [(i, (i + 1) % size) for i in range(size)]
    backward = [(target, source) for source, target in forward]
    return lax.ppermute(low, axis, forward), lax.ppermute(high, axis, backward)


def shards(populations, displacement, offsets, cell_local, destination, triangles, stiffness):
    tiles = lax.axis_size("gx") * lax.axis_size("gy")
    dest_rows = destination.reshape(-1, LANES)
    packed, slot = sender(
        displacement,
        offsets,
        cell_local,
        dest_rows,
        triangles.T,
        stiffness.reshape(-1, LANES),
        tiles,
    )
    arrived = to_all(packed, tiles)
    field, spans, moved, x_plus, x_minus, y_plus, y_minus = fluid(arrived, populations)
    sums = gather(arrived, field, spans)
    x_plus, x_minus = both_ways("gx", x_plus, x_minus)
    moved, y_plus, y_minus, sums = patch_x(moved, x_plus, x_minus, y_plus, y_minus, sums)
    returned = to_all(sums, tiles)
    y_plus, y_minus = both_ways("gy", y_plus, y_minus)
    populations_next, done = patch_y(moved, y_plus, y_minus)
    marker_velocity = unpack(returned, dest_rows, slot, done)
    return (populations_next, marker_velocity)


def solution(mesh):
    return jax.shard_map(
        shards,
        mesh=mesh,
        in_specs=(
            P(None, "gx", "gy", None),
            P(None, ("gx", "gy")),
            P(None, ("gx", "gy")),
            P(None, ("gx", "gy")),
            P(("gx", "gy"), None),
            P(("gx", "gy"), None),
            P(("gx", "gy")),
        ),
        out_specs=(P(None, "gx", "gy", None), P(None, ("gx", "gy"))),
        check_vma=False,
    )
```
